128 devices in a mesh: row: 16 (over y_hi, x, core), col: 8 (over y_lo, z).
Axes of the slice: x: 4, y: 4 (y_hi: 2, y_lo: 2; y = y_hi * 2 + y_lo), z: 4, core: 2. Of those that a mesh axis runs over, the one named last changes fastest.
Arguments:
- inputs: bfloat16 [1024, 12288], P('col', 'row'), may hold values from -6 to 6
- weight: bfloat16 [12288, 49152], P('row', 'col'), may hold values from -0.0546875 to 0.0546875
- cotangent: bfloat16 [1024, 49152], P('row', 'col'), may hold values from -6 to 6
Outputs:
- activated: bfloat16 [1024, 49152], P('row', 'col')
- grad_input: bfloat16 [1024, 12288], P('col', 'row')
- grad_weight: bfloat16 [12288, 49152], P('row', 'col')
The draws below stay inside these ranges and needn't reach their ends.
All inputs are finite; a program needn't handle non-finite values.
Results may differ from the reference program's by a relative error of at most 0.022.
Values may be sent and summed in bfloat16 or wider, within the bound.
A program may use at most 128 MiB of HBM per device.

```python
import jax
import jax.numpy as jnp
from jax import lax

D = 12288
FF = 49152
TOKENS = 1024
N_ROW = 16


def shard_levels(stream_key, shape, split, low, high):
    gain = 1.0
    for position, blocks in split:
        heights = jax.random.uniform(jax.random.fold_in(jax.random.fold_in(stream_key, 6), position), (blocks,), jnp.float32, low / len(split), high / len(split))
        gain = gain * jnp.repeat(jnp.exp(heights), shape[position] // blocks).reshape((-1,) + (1,) * (len(shape) - 1 - position))
    return gain


def bell_draw(rng, extent, scale, most, shards=(), dtype=jnp.bfloat16):
    entries = jax.random.normal(rng, extent, jnp.float32) * scale
    if len(shards) > 0:
        entries = shard_levels(rng, extent, shards, -0.22, 0.18) * entries
    return jnp.clip(entries, min=-most, max=most).astype(dtype)


def setup_inputs(seed: int = 0) -> dict:
    streams_of = jax.random.split(jax.random.key(seed), 4)
    return {
        "inputs": bell_draw(streams_of[0], (TOKENS, D), 1.0, 6.0, ((0, 8), (1, 16))),
        "weight": bell_draw(streams_of[1], (D, FF), D ** -0.5, 0.0546875, ((0, 16), (1, 8))),
        "cotangent": bell_draw(streams_of[2], (TOKENS, FF), 1.0, 6.0, ((0, 16), (1, 8))),
    }


root_coef = 0.7978845608
cube_coef = 0.044715


def gelu_value(pre):
    inner = root_coef * (pre + cube_coef * pre * pre * pre)
    return 0.5 * pre * (1.0 + jnp.tanh(inner))


def gelu_slope(pre):
    tangent = jnp.tanh(root_coef * (pre + cube_coef * pre * pre * pre))
    return 0.5 * (1.0 + tangent) + 0.5 * pre * (1.0 - tangent * tangent) * root_coef * (1.0 + 3.0 * cube_coef * pre * pre)


def reference(inputs, weight, cotangent):
    width = D // N_ROW
    input_blocks = jnp.transpose(inputs.reshape(TOKENS, N_ROW, width), (1, 0, 2))
    weight_blocks = weight.reshape(N_ROW, width, FF)

    def accumulate(total, pair):
        partial_prod = jnp.dot(pair[0], pair[1], preferred_element_type=jnp.float32)
        return total + partial_prod.astype(jnp.bfloat16).astype(jnp.float32), None

    pre, unused = lax.scan(accumulate, jnp.zeros((TOKENS, FF), jnp.float32), (input_blocks, weight_blocks))
    activated = gelu_value(pre).astype(jnp.bfloat16)
    grad_pre = (cotangent.astype(jnp.float32) * gelu_slope(pre)).astype(jnp.bfloat16)
    grad_input = lax.dot_general(grad_pre, weight, (((1,), (1,)), ((), ())), preferred_element_type=jnp.float32).astype(jnp.bfloat16)
    grad_weight = lax.dot_general(inputs, grad_pre, (((0,), (0,)), ((), ())), preferred_element_type=jnp.float32).astype(jnp.bfloat16)
    return activated, grad_input, grad_weight
```

```python
import jax
import jax.numpy as jnp
from jax import lax
from jax.experimental import pallas as pl
from jax.experimental.pallas import tpu as pltpu
from jax.sharding import PartitionSpec as P

MESH = pl.DeviceIdType.MESH
F32 = jnp.float32
BF16 = jnp.bfloat16

root_coef = 0.7978845608
cube_coef = 0.044715

CHUNKS = 4
ROWS = 16
WIDTH = 768
COLS = 6144
TILE = 512
A_COLS = 2560
B_COLS = COLS - A_COLS
A = slice(0, A_COLS)
B = slice(A_COLS, COLS)

NAMES = (
    ["xy", "cA", "cB", "sBy", "sAy", "gAy", "gBy", "gc", "iy"]
    + [f"{n}{d}" for n in ("xz", "xf", "sAx", "sBx", "gAx", "gBx", "gAf", "gBf", "iz") for d in (1, 2, 3)]
)
SLOT = {name: i for i, name in enumerate(NAMES)}


def kernel(
    x_ref, w_hbm, cot_ref,
    act_ref, gi_ref, g_hbm, x_out,
    w, xs, part, share, ra, ta, ray, rb, tb, rbx, grad, acc, gi, rz, ti, ry,
    send_sem, recv_sem, local_sem,
):
    row, col = lax.axis_index("row"), lax.axis_index("col")
    yhi, x, core = row // 8, (row // 2) % 4, row % 2
    ylo, z = col // 4, col % 4

    def device(yhi=yhi, x=x, core=core, ylo=ylo, z=z):
        return (yhi * 8 + x * 2 + core, ylo * 4 + z)

    y_peer = device(yhi=1 - yhi)
    core_peer = device(core=1 - core)
    ylo_peer = device(ylo=1 - ylo)
    x_at = {d: lax.rem(x + d, 4) for d in (1, 2, 3)}
    z_at = {d: lax.rem(z + d, 4) for d in (1, 2, 3)}
    x_peer = {d: device(x=x_at[d]) for d in (1, 2, 3)}
    z_peer = {d: device(z=z_at[d]) for d in (1, 2, 3)}
    peers = [y_peer, core_peer, ylo_peer, *x_peer.values(), *z_peer.values()]

    load_w = pltpu.make_async_copy(w_hbm, w, local_sem.at[0])
    load_w.start()

    barrier = pltpu.get_barrier_semaphore()
    for peer in peers:
        pl.semaphore_signal(barrier, inc=1, device_id=peer, device_id_type=MESH)
    pl.semaphore_wait(barrier, len(peers))

    copies = {}

    def send(k, name, src, dst, peer):
        copy = pltpu.make_async_remote_copy(
            src_ref=src, dst_ref=dst,
            send_sem=send_sem.at[k, SLOT[name]], recv_sem=recv_sem.at[k, SLOT[name]],
            device_id=peer, device_id_type=MESH,
        )
        copy.start()
        copies[k, name] = copy

    def arrived(k, *names):
        for name in names:
            copies[k, name].wait_recv()

    def three(name):
        return [f"{name}{d}" for d in (1, 2, 3)]

    def x_start(k):
        xs[k, :, col] = x_ref[:, k]
        send(k, "xy", x_ref.at[:, k], xs.at[k, :, col], ylo_peer)
        for d in (1, 2, 3):
            send(k, f"xz{d}", x_ref.at[:, k], xs.at[k, :, col], z_peer[d])

    def x_forward(k):
        arrived(k, "xy")
        other = (1 - ylo) * 4 + z
        for d in (1, 2, 3):
            send(k, f"xf{d}", xs.at[k, :, other], xs.at[k, :, other], z_peer[d])

    def tiles(first, last, body):
        @pl.loop(first, last)
        def _(j):
            body(pl.ds(pl.multiple_of(j * TILE, TILE), TILE))

    def product(k):
        arrived(k, *three("xz"), *three("xf"))
        if k >= 2:
            copies[k - 2, "cA"].wait_send()
            copies[k - 2, "cB"].wait_send()
        lhs = xs.at[k]

        def body(cols):
            out = jnp.dot(lhs[...].reshape(256, WIDTH), w[:, cols], preferred_element_type=F32)
            part[k % 2, :, :, :, cols] = out.astype(BF16).reshape(2, 8, ROWS, TILE)

        tiles(A_COLS // TILE, COLS // TILE, body)
        send(k, "cB", part.at[k % 2, 1 - core, :, :, B], share.at[k, :, :, B], core_peer)
        tiles(0, A_COLS // TILE, body)
        send(k, "cA", part.at[k % 2, 1 - core, :, :, A], share.at[k, :, :, A], core_peer)

    def reduce_first(k):
        def body(cols):
            mine = part[k % 2, core, :, :, cols].astype(F32)
            share[k, :, :, cols] = (mine + share[k, :, :, cols].astype(F32)).astype(BF16)

        arrived(k, "cB")
        tiles(A_COLS // TILE, COLS // TILE, body)
        send(k, "sBy", share.at[k, pl.ds((1 - yhi) * 4, 4), :, B], rb.at[k], y_peer)
        arrived(k, "cA")
        tiles(0, A_COLS // TILE, body)
        for d in (1, 2, 3):
            send(k, f"sAx{d}", share4(k).at[:, x_at[d], :, A], ra.at[k, d - 1], x_peer[d])

    def share4(k):
        return share.at[k].reshape(2, 4, ROWS, COLS)

    def reduce_second(k):
        arrived(k, "sBy")

        def body_b(j):
            cols = pl.ds(pl.multiple_of(A_COLS + j * TILE, TILE), TILE)
            here = pl.ds(pl.multiple_of(j * TILE, TILE), TILE)
            mine = share[k, pl.ds(yhi * 4, 4), :, cols].astype(F32)
            tb[k, :, :, here] = (mine + rb[k, :, :, here].astype(F32)).astype(BF16)

        pl.loop(0, B_COLS // TILE)(body_b)
        for d in (1, 2, 3):
            send(k, f"sBx{d}", tb.at[k, x_at[d]], rbx.at[k, d - 1], x_peer[d])
        arrived(k, *three("sAx"))

        def body_a(cols):
            for h in (0, 1):
                total = share[k, h * 4 + x, :, cols].astype(F32)
                for d in range(3):
                    total += ra[k, d, h, :, cols].astype(F32)
                ta[k, h, :, cols] = total.astype(BF16)

        tiles(0, A_COLS // TILE, body_a)
        send(k, "sAy", ta.at[k, 1 - yhi], ray.at[k], y_peer)

    def activate(k, pre, cols):
        tangent = jnp.tanh(root_coef * (pre + cube_coef * pre * pre * pre))
        act_ref[k, :, cols] = (0.5 * pre * (1.0 + tangent)).astype(BF16)
        slope = 0.5 * (1.0 + tangent) + 0.5 * pre * (1.0 - tangent * tangent) * root_coef * (
            1.0 + 3.0 * cube_coef * pre * pre
        )
        grad[k, core, row // 2, :, cols] = (cot_ref[k, :, cols].astype(F32) * slope).astype(BF16)

    def finish(k):
        arrived(k, "sAy")

        def body_a(cols):
            activate(k, ta[k, yhi, :, cols].astype(F32) + ray[k, :, cols].astype(F32), cols)

        tiles(0, A_COLS // TILE, body_a)
        mine = grad.at[k, core, row // 2]
        send(k, "gAy", mine.at[:, A], mine.at[:, A], y_peer)
        for d in (1, 2, 3):
            send(k, f"gAx{d}", mine.at[:, A], mine.at[:, A], x_peer[d])
        arrived(k, *three("sBx"))

        def body_b(j):
            cols = pl.ds(pl.multiple_of(A_COLS + j * TILE, TILE), TILE)
            here = pl.ds(pl.multiple_of(j * TILE, TILE), TILE)
            pre = tb[k, x, :, here].astype(F32)
            for d in range(3):
                pre += rbx[k, d, :, here].astype(F32)
            activate(k, pre, cols)

        pl.loop(0, B_COLS // TILE)(body_b)
        send(k, "gBy", mine.at[:, B], mine.at[:, B], y_peer)
        for d in (1, 2, 3):
            send(k, f"gBx{d}", mine.at[:, B], mine.at[:, B], x_peer[d])

    def gather_forward(k):
        arrived(k, "gAy")
        block = grad.at[k, core, (1 - yhi) * 4 + x, :, A]
        for d in (1, 2, 3):
            send(k, f"gAf{d}", block, block, x_peer[d])
        for d in (1, 3, 2):
            arrived(k, f"gBx{d}")
            block = grad.at[k, core, yhi * 4 + lax.rem(x + 4 - d, 4), :, B]
            send(k, f"gBf{d}", block, block, y_peer)

    def gather_core(k):
        arrived(k, "gBy", *three("gAx"), *three("gAf"), *three("gBf"))
        send(k, "gc", grad.at[k, core], grad.at[k, core], core_peer)

    stores = []

    def back(k):
        arrived(k, "gc")
        store = pltpu.make_async_copy(grad.at[k], g_hbm.at[k], local_sem.at[1 + k])
        store.start()
        stores.append(store)
        acc[...] = jnp.zeros_like(acc)

        def body(cols):
            acc[...] += lax.dot_general(
                grad[k, :, :, :, cols].reshape(256, TILE), w[:, cols],
                (((1,), (1,)), ((), ())), preferred_element_type=F32,
            )

        tiles(0, COLS // TILE, body)
        gi[k] = acc[...].astype(BF16).reshape(2, 2, 4, ROWS, WIDTH)
        for d in (1, 3, 2):
            send(k, f"iz{d}", gi.at[k, :, :, z_at[d]], rz.at[k, d - 1], z_peer[d])

    def back_second(k):
        arrived(k, *three("iz"))
        total = gi[k, :, :, z].astype(F32)
        for d in range(3):
            total += rz[k, d].astype(F32)
        ti[k] = total.astype(BF16)
        send(k, "iy", ti.at[k, :, 1 - ylo], ry.at[k], ylo_peer)

    def back_third(k):
        arrived(k, "iy")
        gi_ref[:, k] = (ti[k, :, ylo].astype(F32) + ry[k].astype(F32)).astype(BF16)

    for k in range(CHUNKS):
        x_start(k)
    x_forward(0)
    load_w.wait()
    product(0)
    x_forward(1)
    reduce_first(0)
    product(1)
    x_forward(2)
    reduce_second(0)
    reduce_first(1)
    finish(0)
    product(2)
    x_forward(3)
    reduce_second(1)
    reduce_first(2)
    gather_forward(0)
    finish(1)
    product(3)
    gather_core(0)
    reduce_second(2)
    reduce_first(3)
    gather_forward(1)
    back(0)
    finish(2)
    gather_core(1)
    reduce_second(3)
    gather_forward(2)
    back_second(0)
    back(1)
    finish(3)
    gather_core(2)
    gather_forward(3)
    back_third(0)
    back_second(1)
    back(2)
    gather_core(3)
    back_third(1)
    back_second(2)
    x_store = pltpu.make_async_copy(xs, x_out, local_sem.at[5])
    x_store.start()
    back(3)
    back_third(2)
    back_second(3)
    back_third(3)
    x_store.wait()
    for store in stores:
        store.wait()
    for (k, name), copy in copies.items():
        if not (name in ("cA", "cB") and k < 2):
            copy.wait_send()


def exchange(inputs, weight, cotangent):
    vmem = pl.BlockSpec(memory_space=pltpu.VMEM)
    hbm = pl.BlockSpec(memory_space=pl.ANY)
    n = len(NAMES)
    return pl.pallas_call(
        kernel,
        out_shape=(
            jax.ShapeDtypeStruct((CHUNKS, ROWS, COLS), BF16),
            jax.ShapeDtypeStruct((2, CHUNKS, ROWS, WIDTH), BF16),
            jax.ShapeDtypeStruct((CHUNKS, 2, 8, ROWS, COLS), BF16),
            jax.ShapeDtypeStruct((CHUNKS, 2, 8, ROWS, WIDTH), BF16),
        ),
        in_specs=[vmem, hbm, vmem],
        out_specs=(vmem, vmem, hbm, hbm),
        scratch_shapes=[
            pltpu.VMEM((WIDTH, COLS), BF16),
            pltpu.VMEM((CHUNKS, 2, 8, ROWS, WIDTH), BF16),
            pltpu.VMEM((2, 2, 8, ROWS, COLS), BF16),
            pltpu.VMEM((CHUNKS, 8, ROWS, COLS), BF16),
            pltpu.VMEM((CHUNKS, 3, 2, ROWS, A_COLS), BF16),
            pltpu.VMEM((CHUNKS, 2, ROWS, A_COLS), BF16),
            pltpu.VMEM((CHUNKS, ROWS, A_COLS), BF16),
            pltpu.VMEM((CHUNKS, 4, ROWS, B_COLS), BF16),
            pltpu.VMEM((CHUNKS, 4, ROWS, B_COLS), BF16),
            pltpu.VMEM((CHUNKS, 3, ROWS, B_COLS), BF16),
            pltpu.VMEM((CHUNKS, 2, 8, ROWS, COLS), BF16),
            pltpu.VMEM((256, WIDTH), F32),
            pltpu.VMEM((CHUNKS, 2, 2, 4, ROWS, WIDTH), BF16),
            pltpu.VMEM((CHUNKS, 3, 2, 2, ROWS, WIDTH), BF16),
            pltpu.VMEM((CHUNKS, 2, 2, ROWS, WIDTH), BF16),
            pltpu.VMEM((CHUNKS, 2, ROWS, WIDTH), BF16),
            pltpu.SemaphoreType.DMA((CHUNKS, n)),
            pltpu.SemaphoreType.DMA((CHUNKS, n)),
            pltpu.SemaphoreType.DMA((6,)),
        ],
        compiler_params=pltpu.CompilerParams(
            collective_id=0, has_side_effects=True, vmem_limit_bytes=60 * 2**20
        ),
        cost_estimate=pl.CostEstimate(flops=2 * 2 * 1024 * WIDTH * COLS, bytes_accessed=40 * 2**20, transcendentals=0),
        name="exchange",
    )(inputs.reshape(2, CHUNKS, ROWS, WIDTH), weight, cotangent.reshape(CHUNKS, ROWS, COLS))


def shards(inputs, weight, cotangent):
    activated, grad_input, grads, tokens = exchange(inputs, weight, cotangent)
    grad_weight = lax.dot_general(
        tokens.reshape(1024, WIDTH), grads.reshape(1024, COLS),
        (((0,), (0,)), ((), ())), preferred_element_type=F32,
    ).astype(BF16)
    return activated.reshape(64, COLS), grad_input.reshape(128, WIDTH), grad_weight


def solution(mesh):
    return jax.shard_map(
        shards,
        mesh=mesh,
        in_specs=(P("col", "row"), P("row", "col"), P("row", "col")),
        out_specs=(P("row", "col"), P("col", "row"), P("row", "col")),
        check_vma=False,
    )
```

```python
import jax
import jax.numpy as jnp
from jax import lax
from jax.experimental import pallas as pl
from jax.experimental.pallas import tpu as pltpu
from jax.sharding import PartitionSpec as P

MESH = pl.DeviceIdType.MESH
F32 = jnp.float32
BF16 = jnp.bfloat16

root_coef = 0.7978845608
cube_coef = 0.044715

CHUNKS = 4
ROWS = 16
WIDTH = 768
COLS = 6144
TILE = 512
A_COLS = 3584
B_COLS = COLS - A_COLS
A = slice(0, A_COLS)
B = slice(A_COLS, COLS)
A_HALF = (slice(0, 1536), slice(1536, A_COLS))
B_HALF = (slice(0, 1536), slice(1536, B_COLS))
A_WIDE = 2048
B_WIDE = 1536
GROUP = 1024
WAYS = (0, 1)
HOPS = (1, 2, 3)
SLOTS = 56


def width(cols):
    return cols.stop - cols.start


def in_b(cols):
    return slice(A_COLS + cols.start, A_COLS + cols.stop)


def kernel(
    x_ref, w_hbm, cot_ref,
    act_ref, gi_ref, gw_hbm, g_out, x_out,
    w, xs, xt, xt_last, part, share, ah, ra, ta, ay, rb, tb, bh, rbx, grad, acc, gi, rz, rd, ti, ry, stage,
    send_sem, recv_sem, local_sem,
):
    row, col = lax.axis_index("row"), lax.axis_index("col")
    yhi, x, core = row // 8, (row // 2) % 4, row % 2
    ylo, z = col // 4, col % 4
    me = row // 2

    def device(yhi=yhi, x=x, core=core, ylo=ylo, z=z):
        return (yhi * 8 + x * 2 + core, ylo * 4 + z)

    y_peer = device(yhi=1 - yhi)
    core_peer = device(core=1 - core)
    ylo_peer = device(ylo=1 - ylo)
    near = (lax.rem(x + 1, 4), lax.rem(x + 3, 4))
    far = lax.rem(x + 2, 4)
    x_peer = tuple(device(x=at) for at in near)
    z_at = {d: lax.rem(z + d, 4) for d in HOPS}
    z_peer = {d: device(z=z_at[d]) for d in HOPS}
    both_peer = {d: device(ylo=1 - ylo, z=z_at[d]) for d in HOPS}
    peers = [y_peer, core_peer, ylo_peer, *x_peer, *z_peer.values(), *both_peer.values()]

    load_w = pltpu.make_async_copy(w_hbm, w, local_sem.at[0])
    load_w.start()

    barrier = pltpu.get_barrier_semaphore()
    for peer in peers:
        pl.semaphore_signal(barrier, inc=1, device_id=peer, device_id_type=MESH)
    pl.semaphore_wait(barrier, len(peers))

    copies = {}
    slots = [0] * CHUNKS
    unsent = {}
    stores = []
    gw_stores = []

    def send(k, name, src, dst, peer):
        slot = slots[k]
        slots[k] += 1
        copy = pltpu.make_async_remote_copy(
            src_ref=src, dst_ref=dst, send_sem=send_sem.at[k, slot], recv_sem=recv_sem.at[k, slot],
            device_id=peer, device_id_type=MESH,
        )
        copy.start()
        copies[k, name] = unsent[k, name] = copy

    def sent(k, *names):
        for name in names:
            unsent.pop((k, name)).wait_send()

    def arrived(k, *names):
        for name in names:
            copies[k, name].wait_recv()

    def each(name, of):
        return [(name, d) for d in of]

    def tiles(first, last, body):
        @pl.loop(first // TILE, last // TILE)
        def _(j):
            body(pl.ds(pl.multiple_of(j * TILE, TILE), TILE))

    def rows4(k):
        return share.at[k].reshape(2, 4, ROWS, COLS)

    def x_start(k):
        xs[k, :, col] = x_ref[:, k]
        send(k, "xy", x_ref.at[:, k], xs.at[k, :, col], ylo_peer)
        for d in (1, 3, 2):
            send(k, ("xz", d), x_ref.at[:, k], xs.at[k, :, col], z_peer[d])
        if k == 0:
            for d in (1, 3, 2):
                send(k, ("xf", d), x_ref.at[:, k], xs.at[k, :, col], both_peer[d])

    def x_forward(k):
        arrived(k, "xy")
        block = xs.at[k, :, (1 - ylo) * 4 + z]
        for d in (1, 3, 2):
            send(k, ("xf", d), block, block, z_peer[d])

    waited = set()

    def prod_a(k, h):
        product(k, ("cA", h), A_HALF[h])

    def prod_b(k, h):
        product(k, ("cB", h), in_b(B_HALF[h]))

    def product(k, name, cols):
        if not waited:
            load_w.wait()
        if k not in waited:
            waited.add(k)
            arrived(k, *(["xy"] if k == 0 else []), *each("xz", HOPS), *each("xf", HOPS))
        if k >= 2:
            sent(k - 2, name)

        def body(tile):
            out = jnp.dot(xs[k].reshape(256, WIDTH), w[:, tile], preferred_element_type=F32)
            part[k % 2, :, :, :, tile] = out.astype(BF16).reshape(2, 8, ROWS, TILE)

        tiles(cols.start, cols.stop, body)
        send(k, name, part.at[k % 2, 1 - core, :, :, cols], share.at[k, :, :, cols], core_peer)

    def add_cores(k, name, cols):
        arrived(k, name)

        def body(tile):
            mine = part[k % 2, core, :, :, tile].astype(F32)
            share[k, :, :, tile] = (mine + share[k, :, :, tile].astype(F32)).astype(BF16)

        tiles(cols.start, cols.stop, body)

    def ra1(k, h):
        cols = A_HALF[h]
        add_cores(k, ("cA", h), cols)
        n = width(cols)
        send(k, ("ah", h), rows4(k).at[:, far, :, cols], ah.at[k, h, :, :, 0:n], x_peer[h])
        send(k, ("an", 1 - h), rows4(k).at[:, near[1 - h], :, cols], ra.at[k, 1 - h, :, :, cols], x_peer[1 - h])

    def ra2(k, h):
        cols = A_HALF[h]
        arrived(k, ("ah", h))
        for y in (0, 1):
            at = y * 4 + near[h]
            total = share[k, at, :, cols].astype(F32) + ah[k, h, y, :, 0 : width(cols)].astype(F32)
            share[k, at, :, cols] = total.astype(BF16)
        send(k, ("am", h), rows4(k).at[:, near[h], :, cols], ra.at[k, h, :, :, cols], x_peer[h])

    def ra3(k):
        arrived(k, *each("an", WAYS), *each("am", WAYS))

        def body(tile):
            for y in (0, 1):
                total = share[k, y * 4 + x, :, tile].astype(F32)
                total += ra[k, 0, y, :, tile].astype(F32) + ra[k, 1, y, :, tile].astype(F32)
                ta[k, y, :, tile] = total.astype(BF16)

        tiles(0, A_COLS, body)
        send(k, "ay", ta.at[k, 1 - yhi], ay.at[k], y_peer)

    def rb1(k, h):
        cols = B_HALF[h]
        add_cores(k, ("cB", h), in_b(cols))
        send(k, ("by", h), share.at[k, pl.ds((1 - yhi) * 4, 4), :, in_b(cols)], rb.at[k, :, :, cols], y_peer)

    def rb2(k, h):
        cols = B_HALF[h]
        arrived(k, ("by", h))
        for at in range(4):
            total = share[k, yhi * 4 + at, :, in_b(cols)].astype(F32) + rb[k, at, :, cols].astype(F32)
            tb[k, at, :, cols] = total.astype(BF16)
        send(k, ("bh", h), tb.at[k, far, :, cols], bh.at[k, h, :, 0 : width(cols)], x_peer[h])
        send(k, ("bn", 1 - h), tb.at[k, near[1 - h], :, cols], rbx.at[k, 1 - h, :, cols], x_peer[1 - h])

    def rb3(k, h):
        cols = B_HALF[h]
        arrived(k, ("bh", h))
        total = tb[k, near[h], :, cols].astype(F32) + bh[k, h, :, 0 : width(cols)].astype(F32)
        tb[k, near[h], :, cols] = total.astype(BF16)
        send(k, ("bm", h), tb.at[k, near[h], :, cols], rbx.at[k, h, :, cols], x_peer[h])

    def activate(k, pre, cols):
        tangent = jnp.tanh(root_coef * (pre + cube_coef * pre * pre * pre))
        act_ref[k, :, cols] = (0.5 * pre * (1.0 + tangent)).astype(BF16)
        slope = 0.5 * (1.0 + tangent) + 0.5 * pre * (1.0 - tangent * tangent) * root_coef * (
            1.0 + 3.0 * cube_coef * pre * pre
        )
        grad[k, core, me, :, cols] = (cot_ref[k, :, cols].astype(F32) * slope).astype(BF16)

    def block(k, y, at, cols):
        return grad.at[k, core, y * 4 + at, :, cols]

    def pass_on(k, name, ref, peer):
        send(k, name, ref, ref, peer)

    def fin_a(k):
        arrived(k, "ay")

        def body(tile):
            activate(k, ta[k, yhi, :, tile].astype(F32) + ay[k, :, tile].astype(F32), tile)

        tiles(0, A_COLS, body)
        mine = block(k, yhi, x, A)
        pass_on(k, "gAy", mine, y_peer)
        for h in WAYS:
            pass_on(k, ("gA", h), mine, x_peer[h])

    def fin_b(k):
        arrived(k, *each("bn", WAYS), *each("bm", WAYS))

        @pl.loop(0, B_COLS // TILE)
        def _(j):
            here = pl.ds(pl.multiple_of(j * TILE, TILE), TILE)
            pre = tb[k, x, :, here].astype(F32) + rbx[k, 0, :, here].astype(F32) + rbx[k, 1, :, here].astype(F32)
            activate(k, pre, pl.ds(pl.multiple_of(A_COLS + j * TILE, TILE), TILE))

        mine = block(k, yhi, x, B)
        for h in WAYS:
            pass_on(k, ("gB", h), mine, x_peer[h])
        pass_on(k, "gBy", mine, y_peer)

    def relay(k, name, y, halves):
        for h in WAYS:
            pass_on(k, (name, h), block(k, y, near[1 - h], halves[h]), x_peer[h])

    def ga1(k):
        arrived(k, *each("gA", WAYS))
        relay(k, "gAr", yhi, A_HALF)

    def gp1(k):
        arrived(k, "gAy")
        for h in WAYS:
            pass_on(k, ("gP", h), block(k, 1 - yhi, x, A), x_peer[h])

    def gp2(k):
        arrived(k, *each("gP", WAYS))
        relay(k, "gPr", 1 - yhi, A_HALF)

    def gb1(k):
        arrived(k, *each("gB", WAYS))
        relay(k, "gBr", yhi, [in_b(cols) for cols in B_HALF])
        for h in WAYS:
            pass_on(k, ("gBz", h), block(k, yhi, near[h], B), y_peer)

    def to_core(k, name, y, cols):
        pass_on(k, name, grad.at[k, core, pl.ds(y * 4, 4), :, cols], core_peer)

    def gb2(k):
        arrived(k, *each("gBr", WAYS))
        pass_on(k, "gBy2", block(k, yhi, far, B), y_peer)
        to_core(k, ("oB", 0), yhi, B)

    def ca1(k):
        arrived(k, *each("gAr", WAYS))
        to_core(k, ("oA", 0), yhi, A)

    def ca2(k):
        arrived(k, *each("gPr", WAYS))
        to_core(k, ("oA", 1), 1 - yhi, A)

    def cb2(k):
        arrived(k, "gBy", *each("gBz", WAYS), "gBy2")
        to_core(k, ("oB", 1), 1 - yhi, B)

    def multiply_back(k, first, last):
        def body(tile):
            acc[...] += lax.dot_general(
                grad[k, :, :, :, tile].reshape(256, TILE), w[:, tile],
                (((1,), (1,)), ((), ())), preferred_element_type=F32,
            )

        tiles(first, last, body)

    def gi_b(k):
        arrived(k, *each("oB", WAYS))
        acc[...] = jnp.zeros_like(acc)
        multiply_back(k, A_COLS, COLS)

    def gi_a(k):
        arrived(k, *each("oA", WAYS))
        if k == CHUNKS - 1:
            store = pltpu.make_async_copy(grad.at[k], g_out, local_sem.at[1])
            store.start()
            stores.append(store)
            xt_last[...] = xs[k].reshape(256, WIDTH).T
            store = pltpu.make_async_copy(xt_last, x_out, local_sem.at[8])
            store.start()
            stores.append(store)
        multiply_back(k, 0, A_COLS)
        gi[k] = acc[...].astype(BF16).reshape(2, 2, 4, ROWS, WIDTH)
        if k < CHUNKS - 1:
            for d in (1, 3, 2):
                send(k, ("iz", d), gi.at[k, :, :, z_at[d]], rz.at[k, d - 1], z_peer[d])
        else:
            for d in (2, 1, 3):
                send(k, ("iz", d), gi.at[k, :, ylo, z_at[d]], rd.at[d - 1], z_peer[d])
                send(k, ("id", d), gi.at[k, :, 1 - ylo, z_at[d]], rd.at[2 + d], both_peer[d])
            send(k, "iy", gi.at[k, :, 1 - ylo, z], rd.at[6], ylo_peer)

    def gi2(k):
        arrived(k, *each("iz", HOPS))
        total = gi[k, :, :, z].astype(F32)
        for d in range(3):
            total += rz[k, d].astype(F32)
        ti[k] = total.astype(BF16)
        send(k, "iy", ti.at[k, :, 1 - ylo], ry.at[k], ylo_peer)

    def gi3(k):
        arrived(k, "iy")
        if k < CHUNKS - 1:
            total = ti[k, :, ylo].astype(F32) + ry[k].astype(F32)
        else:
            arrived(k, *each("iz", HOPS), *each("id", HOPS))
            total = gi[k, :, ylo, z].astype(F32)
            for d in range(7):
                total += rd[d].astype(F32)
        gi_ref[:, k] = total.astype(BF16)

    def gw(g):
        slot = g % 2
        if g == 0:
            xt[...] = xs[0 : CHUNKS - 1].reshape(256 * (CHUNKS - 1), WIDTH).T
        if g >= 2:
            gw_stores[g - 2].wait()

        @pl.loop(0, GROUP // TILE)
        def _(j):
            cols = pl.ds(pl.multiple_of(g * GROUP + j * TILE, TILE), TILE)
            out = jnp.dot(
                xt[...], grad[0 : CHUNKS - 1, :, :, :, cols].reshape(256 * (CHUNKS - 1), TILE),
                preferred_element_type=F32,
            )
            stage[slot, :, pl.ds(pl.multiple_of(j * TILE, TILE), TILE)] = out.astype(BF16)

        store = pltpu.make_async_copy(
            stage.at[slot], gw_hbm.at[g], local_sem.at[2 + g]
        )
        store.start()
        gw_stores.append(store)

    x_start(0)
    prod_a(0, 0)
    x_start(1)
    prod_a(0, 1)
    prod_b(0, 0)
    x_forward(1)
    ra1(0, 0)
    prod_b(0, 1)
    x_start(2)
    ra1(0, 1)
    rb1(0, 0)
    rb1(0, 1)
    prod_a(1, 0)
    x_forward(2)
    ra2(0, 0)
    prod_a(1, 1)
    ra2(0, 1)
    x_start(3)
    prod_b(1, 0)
    ra1(1, 0)
    prod_b(1, 1)
    ra1(1, 1)
    prod_a(2, 0)
    rb2(0, 1)
    rb2(0, 0)
    x_forward(3)
    ra3(0)
    rb1(1, 1)
    rb1(1, 0)
    ra2(1, 0)
    prod_a(2, 1)
    ra1(2, 0)
    rb3(0, 1)
    prod_b(2, 0)
    rb3(0, 0)
    prod_b(2, 1)
    ra2(1, 1)
    ra1(2, 1)
    prod_a(3, 0)
    fin_a(0)
    rb1(2, 0)
    rb1(2, 1)
    rb2(1, 1)
    fin_b(0)
    prod_a(3, 1)
    ra1(3, 0)
    ra2(2, 0)
    prod_b(3, 0)
    rb2(1, 0)
    prod_b(3, 1)
    ra1(3, 1)
    rb3(1, 1)
    ra3(1)
    rb1(3, 0)
    rb1(3, 1)
    ra2(2, 1)
    gp1(0)
    gb1(0)
    rb3(1, 0)
    ga1(0)
    rb2(2, 1)
    ra2(3, 0)
    rb3(2, 1)
    gb2(0)
    fin_b(1)
    rb2(2, 0)
    ca1(0)
    fin_a(1)
    ra2(3, 1)
    gp2(0)
    ra3(2)
    rb2(3, 1)
    rb3(2, 0)
    cb2(0)
    rb3(3, 1)
    gb1(1)
    rb2(3, 0)
    fin_b(2)
    ca2(0)
    gp1(1)
    gi_b(0)
    ga1(1)
    fin_a(2)
    gi_a(0)
    rb3(3, 0)
    gb2(1)
    ra3(3)
    gb1(2)
    ca1(1)
    fin_b(3)
    gp1(2)
    gp2(1)
    gi2(0)
    ga1(2)
    gb2(2)
    cb2(1)
    gi_b(1)
    fin_a(3)
    ca2(1)
    gb1(3)
    ca1(2)
    gi3(0)
    gp2(2)
    cb2(2)
    gi_a(1)
    gb2(3)
    ga1(3)
    ca2(2)
    gi_b(2)
    gp1(3)
    ca1(3)
    cb2(3)
    gi_a(2)
    gi2(1)
    gp2(3)
    gw(0)
    gi_b(3)
    ca2(3)
    gi3(1)
    gw(1)
    gi2(2)
    gw(2)
    gi_a(3)
    gi3(2)
    gw(3)
    gw(4)
    gw(5)
    gi3(3)

    for store in stores + gw_stores[-2:]:
        store.wait()
    for copy in unsent.values():
        copy.wait_send()


def exchange(inputs, weight, cotangent):
    vmem = pl.BlockSpec(memory_space=pltpu.VMEM)
    hbm = pl.BlockSpec(memory_space=pl.ANY)
    return pl.pallas_call(
        kernel,
        out_shape=(
            jax.ShapeDtypeStruct((CHUNKS, ROWS, COLS), BF16),
            jax.ShapeDtypeStruct((2, CHUNKS, ROWS, WIDTH), BF16),
            jax.ShapeDtypeStruct((COLS // GROUP, WIDTH, GROUP), BF16),
            jax.ShapeDtypeStruct((2, 8, ROWS, COLS), BF16),
            jax.ShapeDtypeStruct((WIDTH, 256), BF16),
        ),
        in_specs=[vmem, hbm, vmem],
        out_specs=(vmem, vmem, hbm, hbm, hbm),
        scratch_shapes=[
            pltpu.VMEM((WIDTH, COLS), BF16),
            pltpu.VMEM((CHUNKS, 2, 8, ROWS, WIDTH), BF16),
            pltpu.VMEM((WIDTH, 256 * (CHUNKS - 1)), BF16),
            pltpu.VMEM((WIDTH, 256), BF16),
            pltpu.VMEM((2, 2, 8, ROWS, COLS), BF16),
            pltpu.VMEM((CHUNKS, 8, ROWS, COLS), BF16),
            pltpu.VMEM((CHUNKS, 2, 2, ROWS, A_WIDE), BF16),
            pltpu.VMEM((CHUNKS, 2, 2, ROWS, A_COLS), BF16),
            pltpu.VMEM((CHUNKS, 2, ROWS, A_COLS), BF16),
            pltpu.VMEM((CHUNKS, ROWS, A_COLS), BF16),
            pltpu.VMEM((CHUNKS, 4, ROWS, B_COLS), BF16),
            pltpu.VMEM((CHUNKS, 4, ROWS, B_COLS), BF16),
            pltpu.VMEM((CHUNKS, 2, ROWS, B_WIDE), BF16),
            pltpu.VMEM((CHUNKS, 2, ROWS, B_COLS), BF16),
            pltpu.VMEM((CHUNKS, 2, 8, ROWS, COLS), BF16),
            pltpu.VMEM((256, WIDTH), F32),
            pltpu.VMEM((CHUNKS, 2, 2, 4, ROWS, WIDTH), BF16),
            pltpu.VMEM((CHUNKS - 1, 3, 2, 2, ROWS, WIDTH), BF16),
            pltpu.VMEM((7, 2, ROWS, WIDTH), BF16),
            pltpu.VMEM((CHUNKS - 1, 2, 2, ROWS, WIDTH), BF16),
            pltpu.VMEM((CHUNKS - 1, 2, ROWS, WIDTH), BF16),
            pltpu.VMEM((2, WIDTH, GROUP), BF16),
            pltpu.SemaphoreType.DMA((CHUNKS, SLOTS)),
            pltpu.SemaphoreType.DMA((CHUNKS, SLOTS)),
            pltpu.SemaphoreType.DMA((9,)),
        ],
        compiler_params=pltpu.CompilerParams(
            collective_id=0, has_side_effects=True, vmem_limit_bytes=61 * 2**20
        ),
        cost_estimate=pl.CostEstimate(flops=5 * 1024 * WIDTH * COLS, bytes_accessed=24 * 2**20, transcendentals=0),
        name="exchange",
    )(inputs.reshape(2, CHUNKS, ROWS, WIDTH), weight, cotangent.reshape(CHUNKS, ROWS, COLS))


def last_tokens(sum_hbm, x_hbm, g_hbm, o_hbm, total, x_t, grads, sem, out_sem):
    groups = COLS // GROUP
    tokens = pltpu.make_async_copy(x_hbm, x_t, sem.at[0])
    tokens.start()
    loads = []
    for g in range(groups):
        cols = slice(g * GROUP, (g + 1) * GROUP)
        pair = (
            pltpu.make_async_copy(g_hbm.at[:, :, :, cols], grads.at[:, :, :, cols], sem.at[1 + g]),
            pltpu.make_async_copy(sum_hbm.at[g], total.at[g], sem.at[1 + groups + g]),
        )
        for load in pair:
            load.start()
        loads.append(pair)
    tokens.wait()
    stores = []
    for g in range(groups):
        for load in loads[g]:
            load.wait()

        @pl.loop(0, GROUP // TILE)
        def _(j):
            here = pl.ds(pl.multiple_of(j * TILE, TILE), TILE)
            cols = pl.ds(pl.multiple_of(g * GROUP + j * TILE, TILE), TILE)
            more = jnp.dot(
                x_t[...], grads[:, :, :, cols].reshape(256, TILE), preferred_element_type=F32
            )
            total[g, :, here] = (total[g, :, here].astype(F32) + more).astype(BF16)

        store = pltpu.make_async_copy(total.at[g], o_hbm.at[:, g * GROUP : (g + 1) * GROUP], out_sem.at[g])
        store.start()
        stores.append(store)
    for store in stores:
        store.wait()


def add_last(partial, tokens, grads):
    hbm = pl.BlockSpec(memory_space=pl.ANY)
    groups = COLS // GROUP
    return pl.pallas_call(
        last_tokens,
        out_shape=jax.ShapeDtypeStruct((WIDTH, COLS), BF16),
        in_specs=[hbm, hbm, hbm],
        out_specs=hbm,
        scratch_shapes=[
            pltpu.VMEM((groups, WIDTH, GROUP), BF16),
            pltpu.VMEM((WIDTH, 256), BF16),
            pltpu.VMEM((2, 8, ROWS, COLS), BF16),
            pltpu.SemaphoreType.DMA((1 + 2 * groups,)),
            pltpu.SemaphoreType.DMA((groups,)),
        ],
        compiler_params=pltpu.CompilerParams(vmem_limit_bytes=60 * 2**20),
        cost_estimate=pl.CostEstimate(flops=2 * 256 * WIDTH * COLS, bytes_accessed=24 * 2**20, transcendentals=0),
        name="add_last",
    )(partial, tokens, grads)


def shards(inputs, weight, cotangent):
    activated, grad_input, partial, grads, tokens = exchange(inputs, weight, cotangent)
    grad_weight = add_last(partial, tokens, grads)
    return activated.reshape(64, COLS), grad_input.reshape(128, WIDTH), grad_weight


def solution(mesh):
    return jax.shard_map(
        shards,
        mesh=mesh,
        in_specs=(P("col", "row"), P("row", "col"), P("row", "col")),
        out_specs=(P("row", "col"), P("col", "row"), P("row", "col")),
        check_vma=False,
    )
```

```python
import jax
import jax.numpy as jnp
from jax import lax
from jax.experimental import pallas as pl
from jax.experimental.pallas import tpu as pltpu
from jax.sharding import PartitionSpec as P

MESH = pl.DeviceIdType.MESH
F32 = jnp.float32
BF16 = jnp.bfloat16

root_coef = 0.7978845608
cube_coef = 0.044715

CHUNKS = 4
LAST = CHUNKS - 1
ROWS = 16
WIDTH = 768
COLS = 6144
TILE = 512
A_COLS = 3584
B_COLS = COLS - A_COLS
A = slice(0, A_COLS)
B = slice(A_COLS, COLS)
A_HALF = (slice(0, 1536), slice(1536, A_COLS))
B_HALF = (slice(0, 1536), slice(1536, B_COLS))
A_WIDE = 2048
B_WIDE = 1536
GROUP = 1024
WAYS = (0, 1)
HOPS = (1, 2, 3)
SLOTS = 224


def width(cols):
    return cols.stop - cols.start


def in_b(cols):
    return slice(A_COLS + cols.start, A_COLS + cols.stop)


def kernel(
    x_ref, w_hbm, cot_ref,
    act_ref, gi_ref, gw_hbm, g_out, x_out,
    w, xs, xt, xt_last, part, share, ah, ra, ta, ay, rb, tb, bh, rbx, grad, acc, gi, rz, rd, ti, ry, stage,
    send_sem, recv_sem, local_sem,
):
    row, col = lax.axis_index("row"), lax.axis_index("col")
    yhi, x, core = row // 8, (row // 2) % 4, row % 2
    ylo, z = col // 4, col % 4
    me = row // 2

    def device(yhi=yhi, x=x, core=core, ylo=ylo, z=z):
        return (yhi * 8 + x * 2 + core, ylo * 4 + z)

    y_peer = device(yhi=1 - yhi)
    core_peer = device(core=1 - core)
    ylo_peer = device(ylo=1 - ylo)
    near = (lax.rem(x + 1, 4), lax.rem(x + 3, 4))
    far = lax.rem(x + 2, 4)
    x_peer = tuple(device(x=at) for at in near)
    z_at = {d: lax.rem(z + d, 4) for d in HOPS}
    z_peer = {d: device(z=z_at[d]) for d in HOPS}
    both_peer = {d: device(ylo=1 - ylo, z=z_at[d]) for d in HOPS}
    peers = [y_peer, core_peer, ylo_peer, *x_peer, *z_peer.values(), *both_peer.values()]

    load_w = pltpu.make_async_copy(w_hbm, w, local_sem.at[0])
    load_w.start()

    barrier = pltpu.get_barrier_semaphore()
    for peer in peers:
        pl.semaphore_signal(barrier, inc=1, device_id=peer, device_id_type=MESH)
    pl.semaphore_wait(barrier, len(peers))

    copies = {}
    unsent = {}
    stores = []
    gw_stores = []

    def send(k, name, src, dst, peer):
        slot = len(copies)
        copy = pltpu.make_async_remote_copy(
            src_ref=src, dst_ref=dst, send_sem=send_sem.at[slot], recv_sem=recv_sem.at[slot],
            device_id=peer, device_id_type=MESH,
        )
        copy.start()
        copies[k, name] = unsent[k, name] = copy

    def sent(k, *names):
        for name in names:
            unsent.pop((k, name)).wait_send()

    def arrived(k, *names):
        for name in names:
            copies[k, name].wait_recv()

    def each(name, of):
        return [(name, d) for d in of]

    def tiles(first, last, body):
        @pl.loop(first // TILE, last // TILE)
        def _(j):
            body(pl.ds(pl.multiple_of(j * TILE, TILE), TILE))

    def rows4(k):
        return share.at[k].reshape(2, 4, ROWS, COLS)

    def x_start(k):
        xs[k, :, col] = x_ref[:, k]
        send(k, "xy", x_ref.at[:, k], xs.at[k, :, col], ylo_peer)
        for d in (1, 3, 2):
            send(k, ("xz", d), x_ref.at[:, k], xs.at[k, :, col], z_peer[d])
        if k == 0:
            for d in (1, 3, 2):
                send(k, ("xf", d), x_ref.at[:, k], xs.at[k, :, col], both_peer[d])

    def x_forward(k):
        arrived(k, "xy")
        block = xs.at[k, :, (1 - ylo) * 4 + z]
        for d in (1, 3, 2):
            send(k, ("xf", d), block, block, z_peer[d])

    waited = set()

    def prod_a(k, h):
        product(k, ("cA", h), A_HALF[h])

    def prod_b(k, h):
        product(k, ("cB", h), in_b(B_HALF[h]))

    def product(k, name, cols):
        if not waited:
            load_w.wait()
        if k not in waited:
            waited.add(k)
            arrived(k, *(["xy"] if k == 0 else []), *each("xz", HOPS), *each("xf", HOPS))
        if k >= 2:
            sent(k - 2, name)

        def body(tile):
            out = jnp.dot(xs[k].reshape(256, WIDTH), w[:, tile], preferred_element_type=F32)
            part[k % 2, :, :, :, tile] = out.astype(BF16).reshape(2, 8, ROWS, TILE)

        tiles(cols.start, cols.stop, body)
        send(k, name, part.at[k % 2, 1 - core, :, :, cols], share.at[k, :, :, cols], core_peer)

    def add_cores(k, name, cols):
        arrived(k, name)

        def body(tile):
            mine = part[k % 2, core, :, :, tile].astype(F32)
            share[k, :, :, tile] = (mine + share[k, :, :, tile].astype(F32)).astype(BF16)

        tiles(cols.start, cols.stop, body)

    def ra1(k, h):
        cols = A_HALF[h]
        add_cores(k, ("cA", h), cols)
        n = width(cols)
        send(k, ("ah", h), rows4(k).at[:, far, :, cols], ah.at[k, h, :, :, 0:n], x_peer[h])
        send(k, ("an", 1 - h), rows4(k).at[:, near[1 - h], :, cols], ra.at[k, 1 - h, :, :, cols], x_peer[1 - h])

    def ra2(k, h):
        cols = A_HALF[h]
        arrived(k, ("ah", h))
        for y in (0, 1):
            at = y * 4 + near[h]
            total = share[k, at, :, cols].astype(F32) + ah[k, h, y, :, 0 : width(cols)].astype(F32)
            share[k, at, :, cols] = total.astype(BF16)
        send(k, ("am", h), rows4(k).at[:, near[h], :, cols], ra.at[k, h, :, :, cols], x_peer[h])

    def ra3(k):
        arrived(k, *each("an", WAYS), *each("am", WAYS))

        def body(tile):
            for y in (0, 1):
                total = share[k, y * 4 + x, :, tile].astype(F32)
                total += ra[k, 0, y, :, tile].astype(F32) + ra[k, 1, y, :, tile].astype(F32)
                ta[k, y, :, tile] = total.astype(BF16)

        tiles(0, A_COLS, body)
        send(k, "ay", ta.at[k, 1 - yhi], ay.at[k], y_peer)

    def rb1(k, h):
        cols = B_HALF[h]
        add_cores(k, ("cB", h), in_b(cols))
        send(k, ("by", h), share.at[k, pl.ds((1 - yhi) * 4, 4), :, in_b(cols)], rb.at[k, :, :, cols], y_peer)

    def rb2(k, h):
        cols = B_HALF[h]
        arrived(k, ("by", h))
        for at in range(4):
            total = share[k, yhi * 4 + at, :, in_b(cols)].astype(F32) + rb[k, at, :, cols].astype(F32)
            tb[k, at, :, cols] = total.astype(BF16)
        send(k, ("bh", h), tb.at[k, far, :, cols], bh.at[k, h, :, 0 : width(cols)], x_peer[h])
        send(k, ("bn", 1 - h), tb.at[k, near[1 - h], :, cols], rbx.at[k, 1 - h, :, cols], x_peer[1 - h])

    def rb3(k, h):
        cols = B_HALF[h]
        arrived(k, ("bh", h))
        total = tb[k, near[h], :, cols].astype(F32) + bh[k, h, :, 0 : width(cols)].astype(F32)
        tb[k, near[h], :, cols] = total.astype(BF16)
        send(k, ("bm", h), tb.at[k, near[h], :, cols], rbx.at[k, h, :, cols], x_peer[h])

    def activate(k, pre, cols):
        tangent = jnp.tanh(root_coef * (pre + cube_coef * pre * pre * pre))
        act_ref[k, :, cols] = (0.5 * pre * (1.0 + tangent)).astype(BF16)
        slope = 0.5 * (1.0 + tangent) + 0.5 * pre * (1.0 - tangent * tangent) * root_coef * (
            1.0 + 3.0 * cube_coef * pre * pre
        )
        grad[k, core, me, :, cols] = (cot_ref[k, :, cols].astype(F32) * slope).astype(BF16)

    def block(k, y, at, cols):
        return grad.at[k, core, y * 4 + at, :, cols]

    def pass_on(k, name, ref, peer):
        send(k, name, ref, ref, peer)

    def fin_a(k):
        arrived(k, "ay")

        def body(tile):
            activate(k, ta[k, yhi, :, tile].astype(F32) + ay[k, :, tile].astype(F32), tile)

        tiles(0, A_COLS, body)
        mine = block(k, yhi, x, A)
        pass_on(k, "gAy", mine, y_peer)
        for h in WAYS:
            pass_on(k, ("gA", h), mine, x_peer[h])

    def fin_b(k):
        arrived(k, *each("bn", WAYS), *each("bm", WAYS))

        @pl.loop(0, B_COLS // TILE)
        def _(j):
            here = pl.ds(pl.multiple_of(j * TILE, TILE), TILE)
            pre = tb[k, x, :, here].astype(F32) + rbx[k, 0, :, here].astype(F32) + rbx[k, 1, :, here].astype(F32)
            activate(k, pre, pl.ds(pl.multiple_of(A_COLS + j * TILE, TILE), TILE))

        mine = block(k, yhi, x, B)
        for h in WAYS:
            pass_on(k, ("gB", h), mine, x_peer[h])
        pass_on(k, "gBy", mine, y_peer)

    def relay(k, name, y, halves):
        for h in WAYS:
            pass_on(k, (name, h), block(k, y, near[1 - h], halves[h]), x_peer[h])

    def ga1(k):
        arrived(k, *each("gA", WAYS))
        relay(k, "gAr", yhi, A_HALF)

    def gp1(k):
        arrived(k, "gAy")
        for h in WAYS:
            pass_on(k, ("gP", h), block(k, 1 - yhi, x, A), x_peer[h])
        if k == LAST:
            pass_on(k, ("oA", 1), block(k, 1 - yhi, x, A), core_peer)

    def gp2(k):
        arrived(k, *each("gP", WAYS))
        relay(k, "gPr", 1 - yhi, A_HALF)
        if k == LAST:
            for h in WAYS:
                pass_on(k, ("oA", 2 + h), block(k, 1 - yhi, near[h], A), core_peer)

    def gb1(k):
        arrived(k, *each("gB", WAYS))
        relay(k, "gBr", yhi, [in_b(cols) for cols in B_HALF])
        for h in WAYS:
            pass_on(k, ("gBz", h), block(k, yhi, near[h], B), y_peer)

    def to_core(k, name, y, cols):
        pass_on(k, name, grad.at[k, core, pl.ds(y * 4, 4), :, cols], core_peer)

    def gb2(k):
        arrived(k, *each("gBr", WAYS))
        pass_on(k, "gBy2", block(k, yhi, far, B), y_peer)
        to_core(k, ("oB", 0), yhi, B)

    def ca1(k):
        arrived(k, *each("gAr", WAYS))
        to_core(k, ("oA", 0), yhi, A)

    def ca2(k):
        arrived(k, *each("gPr", WAYS))
        if k == LAST:
            pass_on(k, ("oA", 4), block(k, 1 - yhi, far, A), core_peer)
        else:
            to_core(k, ("oA", 1), 1 - yhi, A)

    def cb2(k):
        arrived(k, "gBy", *each("gBz", WAYS), "gBy2")
        to_core(k, ("oB", 1), 1 - yhi, B)

    def multiply_back(k, first, last, cols):
        def body(n):
            at = pl.ds(pl.multiple_of(n * 256, 256), 256)
            out = lax.dot_general(
                grad[k, :, :, :, cols].reshape(256, width(cols)), w[at, cols],
                (((1,), (1,)), ((), ())), preferred_element_type=F32,
            )
            if cols == B:
                acc[k % 2, :, at] = out
            else:
                out += acc[k % 2, :, at]
                gi[k, :, :, :, :, at] = out.astype(BF16).reshape(2, 2, 4, ROWS, 256)

        pl.loop(first, last)(body)

    def gi_b(k):
        arrived(k, *each("oB", WAYS))
        multiply_back(k, 0, WIDTH // 256, B)

    def gi_a(k):
        arrived(k, *each("oA", WAYS if k < LAST else range(5)))
        if k < LAST:
            multiply_back(k, 0, WIDTH // 256, A)
            for d in (1, 3, 2):
                send(k, ("iz", d), gi.at[k, :, :, z_at[d]], rz.at[k, d - 1], z_peer[d])
        else:
            store = pltpu.make_async_copy(grad.at[k], g_out, local_sem.at[1])
            store.start()
            stores.append(store)
            multiply_back(k, 0, 1, A)
            last_out(0, slice(0, 256))

    def gi_c(k):
        multiply_back(k, 1, WIDTH // 256, A)
        last_out(1, slice(256, WIDTH))
        xt_last[...] = xs[k].reshape(256, WIDTH).T
        store = pltpu.make_async_copy(xt_last, x_out, local_sem.at[8])
        store.start()
        stores.append(store)

    def last_out(s, cols):
        k = LAST
        for d in (2, 1, 3):
            send(k, ("iz", d, s), gi.at[k, :, ylo, z_at[d], :, cols], rd.at[d - 1, :, :, cols], z_peer[d])
            send(k, ("id", d, s), gi.at[k, :, 1 - ylo, z_at[d], :, cols], rd.at[2 + d, :, :, cols], both_peer[d])
        send(k, ("iy", s), gi.at[k, :, 1 - ylo, z, :, cols], rd.at[6, :, :, cols], ylo_peer)

    def gi2(k):
        arrived(k, *each("iz", HOPS))
        total = gi[k, :, :, z].astype(F32)
        for d in range(3):
            total += rz[k, d].astype(F32)
        ti[k] = total.astype(BF16)
        send(k, "iy", ti.at[k, :, 1 - ylo], ry.at[k], ylo_peer)

    def gi3(k):
        if k < LAST:
            arrived(k, "iy")
            total = ti[k, :, ylo].astype(F32) + ry[k].astype(F32)
        else:
            for s in WAYS:
                arrived(k, ("iy", s), *[(n, d, s) for n in ("iz", "id") for d in HOPS])
            total = gi[k, :, ylo, z].astype(F32)
            for d in range(7):
                total += rd[d].astype(F32)
        gi_ref[:, k] = total.astype(BF16)

    def gw(g):
        slot = g % 2
        if g == 0:
            xt[...] = xs[0 : CHUNKS - 1].reshape(256 * (CHUNKS - 1), WIDTH).T
        if g >= 2:
            gw_stores[g - 2].wait()

        @pl.loop(0, GROUP // TILE)
        def _(j):
            cols = pl.ds(pl.multiple_of(g * GROUP + j * TILE, TILE), TILE)
            out = jnp.dot(
                xt[...], grad[0 : CHUNKS - 1, :, :, :, cols].reshape(256 * (CHUNKS - 1), TILE),
                preferred_element_type=F32,
            )
            stage[slot, :, pl.ds(pl.multiple_of(j * TILE, TILE), TILE)] = out.astype(BF16)

        store = pltpu.make_async_copy(
            stage.at[slot], gw_hbm.at[g], local_sem.at[2 + g]
        )
        store.start()
        gw_stores.append(store)

    x_start(0)
    x_start(1)
    prod_b(0, 1)
    prod_a(0, 0)
    prod_b(0, 0)
    x_forward(1)
    rb1(0, 1)
    prod_a(0, 1)
    ra1(0, 0)
    x_start(2)
    rb1(0, 0)
    prod_a(1, 0)
    ra1(0, 1)
    prod_b(1, 1)
    rb2(0, 1)
    ra2(0, 0)
    x_forward(2)
    prod_b(1, 0)
    ra1(1, 0)
    prod_a(1, 1)
    rb3(0, 1)
    rb2(0, 0)
    rb1(1, 1)
    x_start(3)
    rb1(1, 0)
    ra2(0, 1)
    prod_b(2, 1)
    prod_b(2, 0)
    prod_a(2, 0)
    rb1(2, 1)
    ra1(1, 1)
    prod_a(2, 1)
    rb1(2, 0)
    ra2(1, 0)
    x_forward(3)
    ra1(2, 0)
    ra3(0)
    rb3(0, 0)
    ra1(2, 1)
    rb2(1, 1)
    ra2(1, 1)
    prod_a(3, 0)
    prod_b(3, 1)
    prod_b(3, 0)
    rb3(1, 1)
    fin_b(0)
    prod_a(3, 1)
    rb1(3, 1)
    ra1(3, 0)
    rb1(3, 0)
    rb2(2, 1)
    rb2(1, 0)
    ra2(2, 0)
    fin_a(0)
    ra1(3, 1)
    ra2(2, 1)
    ra3(1)
    rb3(2, 1)
    gb1(0)
    rb3(1, 0)
    rb2(2, 0)
    ra2(3, 0)
    rb2(3, 1)
    gb2(0)
    fin_b(1)
    gp1(0)
    rb3(2, 0)
    ga1(0)
    ra2(3, 1)
    ra3(2)
    rb3(3, 1)
    fin_a(1)
    rb2(3, 0)
    cb2(0)
    fin_b(2)
    ca1(0)
    gb1(1)
    gi_b(0)
    gp1(1)
    fin_a(2)
    rb3(3, 0)
    gp2(0)
    gb2(1)
    ga1(1)
    ra3(3)
    gb1(2)
    gp1(2)
    fin_b(3)
    cb2(1)
    ca2(0)
    gi_b(1)
    gb2(2)
    ga1(2)
    gp2(1)
    ca1(1)
    gi_a(0)
    gb1(3)
    gp2(2)
    fin_a(3)
    cb2(2)
    ca1(2)
    ca2(1)
    gi_b(2)
    gb2(3)
    ca2(2)
    gi2(0)
    ga1(3)
    gi_a(1)
    gp1(3)
    gi_a(2)
    cb2(3)
    ca1(3)
    gi3(0)
    gw(0)
    gp2(3)
    gw(1)
    gw(2)
    ca2(3)
    gi2(1)
    gi_b(3)
    gi_a(3)
    gi_c(3)
    gi3(1)
    gi2(2)
    gw(3)
    gw(4)
    gw(5)
    gi3(3)
    gi3(2)

    for store in stores + gw_stores[-2:]:
        store.wait()
    for copy in unsent.values():
        copy.wait_send()


def exchange(inputs, weight, cotangent):
    vmem = pl.BlockSpec(memory_space=pltpu.VMEM)
    hbm = pl.BlockSpec(memory_space=pl.ANY)
    return pl.pallas_call(
        kernel,
        out_shape=(
            jax.ShapeDtypeStruct((CHUNKS, ROWS, COLS), BF16),
            jax.ShapeDtypeStruct((2, CHUNKS, ROWS, WIDTH), BF16),
            jax.ShapeDtypeStruct((COLS // GROUP, WIDTH, GROUP), BF16),
            jax.ShapeDtypeStruct((2, 8, ROWS, COLS), BF16),
            jax.ShapeDtypeStruct((WIDTH, 256), BF16),
        ),
        in_specs=[vmem, hbm, vmem],
        out_specs=(vmem, vmem, hbm, hbm, hbm),
        scratch_shapes=[
            pltpu.VMEM((WIDTH, COLS), BF16),
            pltpu.VMEM((CHUNKS, 2, 8, ROWS, WIDTH), BF16),
            pltpu.VMEM((WIDTH, 256 * (CHUNKS - 1)), BF16),
            pltpu.VMEM((WIDTH, 256), BF16),
            pltpu.VMEM((2, 2, 8, ROWS, COLS), BF16),
            pltpu.VMEM((CHUNKS, 8, ROWS, COLS), BF16),
            pltpu.VMEM((CHUNKS, 2, 2, ROWS, A_WIDE), BF16),
            pltpu.VMEM((CHUNKS, 2, 2, ROWS, A_COLS), BF16),
            pltpu.VMEM((CHUNKS, 2, ROWS, A_COLS), BF16),
            pltpu.VMEM((CHUNKS, ROWS, A_COLS), BF16),
            pltpu.VMEM((CHUNKS, 4, ROWS, B_COLS), BF16),
            pltpu.VMEM((CHUNKS, 4, ROWS, B_COLS), BF16),
            pltpu.VMEM((CHUNKS, 2, ROWS, B_WIDE), BF16),
            pltpu.VMEM((CHUNKS, 2, ROWS, B_COLS), BF16),
            pltpu.VMEM((CHUNKS, 2, 8, ROWS, COLS), BF16),
            pltpu.VMEM((2, 256, WIDTH), F32),
            pltpu.VMEM((CHUNKS, 2, 2, 4, ROWS, WIDTH), BF16),
            pltpu.VMEM((CHUNKS - 1, 3, 2, 2, ROWS, WIDTH), BF16),
            pltpu.VMEM((7, 2, ROWS, WIDTH), BF16),
            pltpu.VMEM((CHUNKS - 1, 2, 2, ROWS, WIDTH), BF16),
            pltpu.VMEM((CHUNKS - 1, 2, ROWS, WIDTH), BF16),
            pltpu.VMEM((2, WIDTH, GROUP), BF16),
            pltpu.SemaphoreType.DMA((SLOTS,)),
            pltpu.SemaphoreType.DMA((SLOTS,)),
            pltpu.SemaphoreType.DMA((9,)),
        ],
        compiler_params=pltpu.CompilerParams(
            collective_id=0, has_side_effects=True, vmem_limit_bytes=61 * 2**20
        ),
        cost_estimate=pl.CostEstimate(flops=5 * 1024 * WIDTH * COLS, bytes_accessed=24 * 2**20, transcendentals=0),
        name="exchange",
    )(inputs.reshape(2, CHUNKS, ROWS, WIDTH), weight, cotangent.reshape(CHUNKS, ROWS, COLS))


def last_tokens(
    sum_hbm, x_hbm, g_hbm, act_hbm, gi_hbm, o_hbm, act_out, gi_out,
    total, x_t, grads, act, gi, sem, out_sem,
):
    groups = COLS // GROUP
    tokens = pltpu.make_async_copy(x_hbm, x_t, sem.at[0])
    tokens.start()
    loads = []
    for g in range(groups):
        cols = slice(g * GROUP, (g + 1) * GROUP)
        pair = (
            pltpu.make_async_copy(g_hbm.at[:, :, :, cols], grads.at[:, :, :, cols], sem.at[1 + g]),
            pltpu.make_async_copy(sum_hbm.at[g], total.at[g], sem.at[1 + groups + g]),
        )
        for load in pair:
            load.start()
        loads.append(pair)
    small = (
        (pltpu.make_async_copy(act_hbm, act, sem.at[1 + 2 * groups]), act, act_out),
        (pltpu.make_async_copy(gi_hbm, gi, sem.at[2 + 2 * groups]), gi, gi_out),
    )
    for load, _, _ in small:
        load.start()
    tokens.wait()
    stores = []
    for g in range(groups):
        for load in loads[g]:
            load.wait()

        @pl.loop(0, GROUP // TILE)
        def _(j):
            here = pl.ds(pl.multiple_of(j * TILE, TILE), TILE)
            cols = pl.ds(pl.multiple_of(g * GROUP + j * TILE, TILE), TILE)
            more = jnp.dot(
                x_t[...], grads[:, :, :, cols].reshape(256, TILE), preferred_element_type=F32
            )
            total[g, :, here] = (total[g, :, here].astype(F32) + more).astype(BF16)

        store = pltpu.make_async_copy(total.at[g], o_hbm.at[:, g * GROUP : (g + 1) * GROUP], out_sem.at[g])
        store.start()
        stores.append(store)
    for n, (load, held, out) in enumerate(small):
        load.wait()
        store = pltpu.make_async_copy(held, out, out_sem.at[groups + n])
        store.start()
        stores.append(store)
    for store in stores:
        store.wait()


def add_last(partial, tokens, grads, activated, grad_input):
    hbm = pl.BlockSpec(memory_space=pl.ANY)
    groups = COLS // GROUP
    return pl.pallas_call(
        last_tokens,
        out_shape=(
            jax.ShapeDtypeStruct((WIDTH, COLS), BF16),
            jax.ShapeDtypeStruct(activated.shape, BF16),
            jax.ShapeDtypeStruct(grad_input.shape, BF16),
        ),
        in_specs=[hbm] * 5,
        out_specs=(hbm, hbm, hbm),
        scratch_shapes=[
            pltpu.VMEM((groups, WIDTH, GROUP), BF16),
            pltpu.VMEM((WIDTH, 256), BF16),
            pltpu.VMEM((2, 8, ROWS, COLS), BF16),
            pltpu.VMEM(activated.shape, BF16),
            pltpu.VMEM(grad_input.shape, BF16),
            pltpu.SemaphoreType.DMA((3 + 2 * groups,)),
            pltpu.SemaphoreType.DMA((groups + 2,)),
        ],
        compiler_params=pltpu.CompilerParams(vmem_limit_bytes=60 * 2**20),
        cost_estimate=pl.CostEstimate(flops=2 * 256 * WIDTH * COLS, bytes_accessed=24 * 2**20, transcendentals=0),
        name="add_last",
    )(partial, tokens, grads, activated, grad_input)


def shards(inputs, weight, cotangent):
    activated, grad_input, partial, grads, tokens = exchange(inputs, weight, cotangent)
    grad_weight, activated, grad_input = add_last(partial, tokens, grads, activated, grad_input)
    return activated.reshape(64, COLS), grad_input.reshape(128, WIDTH), grad_weight


def solution(mesh):
    return jax.shard_map(
        shards,
        mesh=mesh,
        in_specs=(P("col", "row"), P("row", "col"), P("row", "col")),
        out_specs=(P("row", "col"), P("col", "row"), P("row", "col")),
        check_vma=False,
    )
```

```python
import jax
import jax.numpy as jnp
from jax import lax
from jax.experimental import pallas as pl
from jax.experimental.pallas import tpu as pltpu
from jax.sharding import PartitionSpec as P

MESH = pl.DeviceIdType.MESH
F32 = jnp.float32
BF16 = jnp.bfloat16

root_coef = 0.7978845608
cube_coef = 0.044715

CHUNKS = 4
LAST = CHUNKS - 1
ROWS = 16
WIDTH = 768
COLS = 6144
TILE = 512
A_COLS = 3584
B_COLS = COLS - A_COLS
A = slice(0, A_COLS)
B = slice(A_COLS, COLS)
A_HALF = (slice(0, 1536), slice(1536, A_COLS))
B_HALF = (slice(0, 1536), slice(1536, B_COLS))
A_WIDE = 2048
B_WIDE = 1536
GROUP = 1024
WAYS = (0, 1)
HOPS = (1, 2, 3)
SLOTS = 224


def width(cols):
    return cols.stop - cols.start


def in_b(cols):
    return slice(A_COLS + cols.start, A_COLS + cols.stop)


def kernel(
    x_hbm, w_hbm, cot_hbm,
    act_out, gi_out, gw_hbm, g_out, x_out,
    w, xs, xt, xt_last, part, share, ah, ra, ta, ay, rb, tb, bh, rbx, grad, acc, gi, rz, rd, ti, ry, stage, cot_ref, act_ref, gi_ref,
    send_sem, recv_sem, local_sem,
):
    row, col = lax.axis_index("row"), lax.axis_index("col")
    yhi, x, core = row // 8, (row // 2) % 4, row % 2
    ylo, z = col // 4, col % 4
    me = row // 2

    def device(yhi=yhi, x=x, core=core, ylo=ylo, z=z):
        return (yhi * 8 + x * 2 + core, ylo * 4 + z)

    y_peer = device(yhi=1 - yhi)
    core_peer = device(core=1 - core)
    ylo_peer = device(ylo=1 - ylo)
    near = (lax.rem(x + 1, 4), lax.rem(x + 3, 4))
    far = lax.rem(x + 2, 4)
    x_peer = tuple(device(x=at) for at in near)
    z_at = {d: lax.rem(z + d, 4) for d in HOPS}
    z_peer = {d: device(z=z_at[d]) for d in HOPS}
    both_peer = {d: device(ylo=1 - ylo, z=z_at[d]) for d in HOPS}
    peers = [y_peer, core_peer, ylo_peer, *x_peer, *z_peer.values(), *both_peer.values()]

    load_x = [
        pltpu.make_async_copy(x_hbm.at[:, k], xs.at[k, :, col], local_sem.at[9 + k]) for k in range(CHUNKS)
    ]
    load_w = pltpu.make_async_copy(w_hbm, w, local_sem.at[0])
    load_cot = pltpu.make_async_copy(cot_hbm, cot_ref, local_sem.at[13])
    for load in (*load_x, load_w, load_cot):
        load.start()

    barrier = pltpu.get_barrier_semaphore()
    for peer in peers:
        pl.semaphore_signal(barrier, inc=1, device_id=peer, device_id_type=MESH)
    pl.semaphore_wait(barrier, len(peers))

    copies = {}
    unsent = {}
    stores = []
    gw_stores = []

    def send(k, name, src, dst, peer):
        slot = len(copies)
        copy = pltpu.make_async_remote_copy(
            src_ref=src, dst_ref=dst, send_sem=send_sem.at[slot], recv_sem=recv_sem.at[slot],
            device_id=peer, device_id_type=MESH,
        )
        copy.start()
        copies[k, name] = unsent[k, name] = copy

    def sent(k, *names):
        for name in names:
            unsent.pop((k, name)).wait_send()

    def arrived(k, *names):
        for name in names:
            copies[k, name].wait_recv()

    def each(name, of):
        return [(name, d) for d in of]

    def tiles(first, last, body):
        @pl.loop(first // TILE, last // TILE)
        def _(j):
            body(pl.ds(pl.multiple_of(j * TILE, TILE), TILE))

    def rows4(k):
        return share.at[k].reshape(2, 4, ROWS, COLS)

    def x_start(k):
        send(k, "xy", x_hbm.at[:, k], xs.at[k, :, col], ylo_peer)
        for d in (1, 3, 2):
            send(k, ("xz", d), x_hbm.at[:, k], xs.at[k, :, col], z_peer[d])
        if k == 0:
            for d in (1, 3, 2):
                send(k, ("xf", d), x_hbm.at[:, k], xs.at[k, :, col], both_peer[d])

    def x_forward(k):
        arrived(k, "xy")
        block = xs.at[k, :, (1 - ylo) * 4 + z]
        for d in (1, 3, 2):
            send(k, ("xf", d), block, block, z_peer[d])

    waited = set()

    def prod_a(k, h):
        product(k, ("cA", h), A_HALF[h])

    def prod_b(k, h):
        product(k, ("cB", h), in_b(B_HALF[h]))

    def product(k, name, cols):
        if not waited:
            load_w.wait()
        if k not in waited:
            waited.add(k)
            load_x[k].wait()
            arrived(k, *(["xy"] if k == 0 else []), *each("xz", HOPS), *each("xf", HOPS))
        if k >= 2:
            sent(k - 2, name)

        def body(tile):
            out = jnp.dot(xs[k].reshape(256, WIDTH), w[:, tile], preferred_element_type=F32)
            part[k % 2, :, :, :, tile] = out.astype(BF16).reshape(2, 8, ROWS, TILE)

        tiles(cols.start, cols.stop, body)
        send(k, name, part.at[k % 2, 1 - core, :, :, cols], share.at[k, :, :, cols], core_peer)

    def add_cores(k, name, cols):
        arrived(k, name)

        def body(tile):
            mine = part[k % 2, core, :, :, tile].astype(F32)
            share[k, :, :, tile] = (mine + share[k, :, :, tile].astype(F32)).astype(BF16)

        tiles(cols.start, cols.stop, body)

    def ra1(k, h):
        cols = A_HALF[h]
        add_cores(k, ("cA", h), cols)
        n = width(cols)
        send(k, ("ah", h), rows4(k).at[:, far, :, cols], ah.at[k, h, :, :, 0:n], x_peer[h])
        send(k, ("an", 1 - h), rows4(k).at[:, near[1 - h], :, cols], ra.at[k, 1 - h, :, :, cols], x_peer[1 - h])

    def ra2(k, h):
        cols = A_HALF[h]
        arrived(k, ("ah", h))
        for y in (0, 1):
            at = y * 4 + near[h]
            total = share[k, at, :, cols].astype(F32) + ah[k, h, y, :, 0 : width(cols)].astype(F32)
            share[k, at, :, cols] = total.astype(BF16)
        send(k, ("am", h), rows4(k).at[:, near[h], :, cols], ra.at[k, h, :, :, cols], x_peer[h])

    def ra3(k):
        arrived(k, *each("an", WAYS), *each("am", WAYS))

        def body(tile):
            for y in (0, 1):
                total = share[k, y * 4 + x, :, tile].astype(F32)
                total += ra[k, 0, y, :, tile].astype(F32) + ra[k, 1, y, :, tile].astype(F32)
                ta[k, y, :, tile] = total.astype(BF16)

        tiles(0, A_COLS, body)
        send(k, "ay", ta.at[k, 1 - yhi], ay.at[k], y_peer)

    def rb1(k, h):
        cols = B_HALF[h]
        add_cores(k, ("cB", h), in_b(cols))
        send(k, ("by", h), share.at[k, pl.ds((1 - yhi) * 4, 4), :, in_b(cols)], rb.at[k, :, :, cols], y_peer)

    def rb2(k, h):
        cols = B_HALF[h]
        arrived(k, ("by", h))
        for at in range(4):
            total = share[k, yhi * 4 + at, :, in_b(cols)].astype(F32) + rb[k, at, :, cols].astype(F32)
            tb[k, at, :, cols] = total.astype(BF16)
        send(k, ("bh", h), tb.at[k, far, :, cols], bh.at[k, h, :, 0 : width(cols)], x_peer[h])
        send(k, ("bn", 1 - h), tb.at[k, near[1 - h], :, cols], rbx.at[k, 1 - h, :, cols], x_peer[1 - h])

    def rb3(k, h):
        cols = B_HALF[h]
        arrived(k, ("bh", h))
        total = tb[k, near[h], :, cols].astype(F32) + bh[k, h, :, 0 : width(cols)].astype(F32)
        tb[k, near[h], :, cols] = total.astype(BF16)
        send(k, ("bm", h), tb.at[k, near[h], :, cols], rbx.at[k, h, :, cols], x_peer[h])

    def activate(k, pre, cols):
        tangent = jnp.tanh(root_coef * (pre + cube_coef * pre * pre * pre))
        act_ref[k, :, cols] = (0.5 * pre * (1.0 + tangent)).astype(BF16)
        slope = 0.5 * (1.0 + tangent) + 0.5 * pre * (1.0 - tangent * tangent) * root_coef * (
            1.0 + 3.0 * cube_coef * pre * pre
        )
        grad[k, core, me, :, cols] = (cot_ref[k, :, cols].astype(F32) * slope).astype(BF16)

    def block(k, y, at, cols):
        return grad.at[k, core, y * 4 + at, :, cols]

    def pass_on(k, name, ref, peer):
        send(k, name, ref, ref, peer)

    activated = []

    def before_activate():
        if not activated:
            load_cot.wait()

    def after_activate(k):
        activated.append(k)
        if activated.count(k) == 2:
            store = pltpu.make_async_copy(act_ref.at[k], act_out.at[k], local_sem.at[14 + k])
            store.start()
            stores.append(store)

    def fin_a(k):
        arrived(k, "ay")
        before_activate()

        def body(tile):
            activate(k, ta[k, yhi, :, tile].astype(F32) + ay[k, :, tile].astype(F32), tile)

        tiles(0, A_COLS, body)
        after_activate(k)
        mine = block(k, yhi, x, A)
        pass_on(k, "gAy", mine, y_peer)
        for h in WAYS:
            pass_on(k, ("gA", h), mine, x_peer[h])

    def fin_b(k):
        arrived(k, *each("bn", WAYS), *each("bm", WAYS))
        before_activate()

        @pl.loop(0, B_COLS // TILE)
        def _(j):
            here = pl.ds(pl.multiple_of(j * TILE, TILE), TILE)
            pre = tb[k, x, :, here].astype(F32) + rbx[k, 0, :, here].astype(F32) + rbx[k, 1, :, here].astype(F32)
            activate(k, pre, pl.ds(pl.multiple_of(A_COLS + j * TILE, TILE), TILE))

        after_activate(k)
        mine = block(k, yhi, x, B)
        for h in WAYS:
            pass_on(k, ("gB", h), mine, x_peer[h])
        pass_on(k, "gBy", mine, y_peer)

    def relay(k, name, y, halves):
        for h in WAYS:
            pass_on(k, (name, h), block(k, y, near[1 - h], halves[h]), x_peer[h])

    def ga1(k):
        arrived(k, *each("gA", WAYS))
        relay(k, "gAr", yhi, A_HALF)

    def gp1(k):
        arrived(k, "gAy")
        for h in WAYS:
            pass_on(k, ("gP", h), block(k, 1 - yhi, x, A), x_peer[h])
        if k == LAST:
            pass_on(k, ("oA", 1), block(k, 1 - yhi, x, A), core_peer)

    def gp2(k):
        arrived(k, *each("gP", WAYS))
        relay(k, "gPr", 1 - yhi, A_HALF)
        if k == LAST:
            for h in WAYS:
                pass_on(k, ("oA", 2 + h), block(k, 1 - yhi, near[h], A), core_peer)

    def gb1(k):
        arrived(k, *each("gB", WAYS))
        relay(k, "gBr", yhi, [in_b(cols) for cols in B_HALF])
        for h in WAYS:
            pass_on(k, ("gBz", h), block(k, yhi, near[h], B), y_peer)

    def to_core(k, name, y, cols):
        pass_on(k, name, grad.at[k, core, pl.ds(y * 4, 4), :, cols], core_peer)

    def gb2(k):
        arrived(k, *each("gBr", WAYS))
        pass_on(k, "gBy2", block(k, yhi, far, B), y_peer)
        to_core(k, ("oB", 0), yhi, B)

    def ca1(k):
        arrived(k, *each("gAr", WAYS))
        to_core(k, ("oA", 0), yhi, A)

    def ca2(k):
        arrived(k, *each("gPr", WAYS))
        if k == LAST:
            pass_on(k, ("oA", 4), block(k, 1 - yhi, far, A), core_peer)
        else:
            to_core(k, ("oA", 1), 1 - yhi, A)

    def cb2(k):
        arrived(k, "gBy", *each("gBz", WAYS), "gBy2")
        to_core(k, ("oB", 1), 1 - yhi, B)

    def multiply_back(k, first, last, cols):
        def body(n):
            at = pl.ds(pl.multiple_of(n * 256, 256), 256)
            out = lax.dot_general(
                grad[k, :, :, :, cols].reshape(256, width(cols)), w[at, cols],
                (((1,), (1,)), ((), ())), preferred_element_type=F32,
            )
            if cols == B:
                acc[k % 2, :, at] = out
            else:
                out += acc[k % 2, :, at]
                gi[k, :, :, :, :, at] = out.astype(BF16).reshape(2, 2, 4, ROWS, 256)

        pl.loop(first, last)(body)

    def gi_b(k):
        arrived(k, *each("oB", WAYS))
        multiply_back(k, 0, WIDTH // 256, B)

    def gi_a(k):
        arrived(k, *each("oA", WAYS if k < LAST else range(5)))
        if k < LAST:
            multiply_back(k, 0, WIDTH // 256, A)
            for d in (1, 3, 2):
                send(k, ("iz", d), gi.at[k, :, :, z_at[d]], rz.at[k, d - 1], z_peer[d])
        else:
            store = pltpu.make_async_copy(grad.at[k], g_out, local_sem.at[1])
            store.start()
            stores.append(store)
            multiply_back(k, 0, 1, A)
            last_out(0, slice(0, 256))

    def gi_c(k):
        multiply_back(k, 1, WIDTH // 256, A)
        last_out(1, slice(256, WIDTH))
        xt_last[...] = xs[k].reshape(256, WIDTH).T
        store = pltpu.make_async_copy(xt_last, x_out, local_sem.at[8])
        store.start()
        stores.append(store)

    def last_out(s, cols):
        k = LAST
        for d in (2, 1, 3):
            send(k, ("iz", d, s), gi.at[k, :, ylo, z_at[d], :, cols], rd.at[d - 1, :, :, cols], z_peer[d])
            send(k, ("id", d, s), gi.at[k, :, 1 - ylo, z_at[d], :, cols], rd.at[2 + d, :, :, cols], both_peer[d])
        send(k, ("iy", s), gi.at[k, :, 1 - ylo, z, :, cols], rd.at[6, :, :, cols], ylo_peer)

    def gi2(k):
        arrived(k, *each("iz", HOPS))
        total = gi[k, :, :, z].astype(F32)
        for d in range(3):
            total += rz[k, d].astype(F32)
        ti[k] = total.astype(BF16)
        send(k, "iy", ti.at[k, :, 1 - ylo], ry.at[k], ylo_peer)

    def gi3(k):
        if k < LAST:
            arrived(k, "iy")
            total = ti[k, :, ylo].astype(F32) + ry[k].astype(F32)
        else:
            for s in WAYS:
                arrived(k, ("iy", s), *[(n, d, s) for n in ("iz", "id") for d in HOPS])
            total = gi[k, :, ylo, z].astype(F32)
            for d in range(7):
                total += rd[d].astype(F32)
        gi_ref[:, k] = total.astype(BF16)
        store = pltpu.make_async_copy(gi_ref.at[:, k], gi_out.at[:, k], local_sem.at[18 + k])
        store.start()
        stores.append(store)

    def gw(g):
        slot = g % 2
        if g == 0:
            xt[...] = xs[0 : CHUNKS - 1].reshape(256 * (CHUNKS - 1), WIDTH).T
        if g >= 2:
            gw_stores[g - 2].wait()

        @pl.loop(0, GROUP // TILE)
        def _(j):
            cols = pl.ds(pl.multiple_of(g * GROUP + j * TILE, TILE), TILE)
            out = jnp.dot(
                xt[...], grad[0 : CHUNKS - 1, :, :, :, cols].reshape(256 * (CHUNKS - 1), TILE),
                preferred_element_type=F32,
            )
            stage[slot, :, pl.ds(pl.multiple_of(j * TILE, TILE), TILE)] = out.astype(BF16)

        store = pltpu.make_async_copy(
            stage.at[slot], gw_hbm.at[g], local_sem.at[2 + g]
        )
        store.start()
        gw_stores.append(store)

    x_start(0)
    x_start(1)
    prod_b(0, 1)
    prod_a(0, 0)
    prod_b(0, 0)
    x_forward(1)
    rb1(0, 1)
    prod_a(0, 1)
    ra1(0, 0)
    x_start(2)
    rb1(0, 0)
    prod_a(1, 0)
    ra1(0, 1)
    prod_b(1, 1)
    rb2(0, 1)
    ra2(0, 0)
    x_forward(2)
    prod_b(1, 0)
    ra1(1, 0)
    prod_a(1, 1)
    rb3(0, 1)
    rb2(0, 0)
    rb1(1, 1)
    x_start(3)
    rb1(1, 0)
    ra2(0, 1)
    prod_b(2, 1)
    prod_b(2, 0)
    prod_a(2, 0)
    rb1(2, 1)
    ra1(1, 1)
    prod_a(2, 1)
    rb1(2, 0)
    ra2(1, 0)
    x_forward(3)
    ra1(2, 0)
    ra3(0)
    rb3(0, 0)
    ra1(2, 1)
    rb2(1, 1)
    ra2(1, 1)
    prod_a(3, 0)
    prod_b(3, 1)
    prod_b(3, 0)
    rb3(1, 1)
    fin_b(0)
    prod_a(3, 1)
    rb1(3, 1)
    ra1(3, 0)
    rb1(3, 0)
    rb2(2, 1)
    rb2(1, 0)
    ra2(2, 0)
    fin_a(0)
    ra1(3, 1)
    ra2(2, 1)
    ra3(1)
    rb3(2, 1)
    gb1(0)
    rb3(1, 0)
    rb2(2, 0)
    ra2(3, 0)
    rb2(3, 1)
    gb2(0)
    fin_b(1)
    gp1(0)
    rb3(2, 0)
    ga1(0)
    ra2(3, 1)
    ra3(2)
    rb3(3, 1)
    fin_a(1)
    rb2(3, 0)
    cb2(0)
    fin_b(2)
    ca1(0)
    gb1(1)
    gi_b(0)
    gp1(1)
    fin_a(2)
    rb3(3, 0)
    gp2(0)
    gb2(1)
    ga1(1)
    ra3(3)
    gb1(2)
    gp1(2)
    fin_b(3)
    cb2(1)
    ca2(0)
    gi_b(1)
    gb2(2)
    ga1(2)
    gp2(1)
    ca1(1)
    gi_a(0)
    gb1(3)
    gp2(2)
    fin_a(3)
    cb2(2)
    ca1(2)
    ca2(1)
    gi_b(2)
    gb2(3)
    ca2(2)
    gi2(0)
    ga1(3)
    gi_a(1)
    gp1(3)
    gi_a(2)
    cb2(3)
    ca1(3)
    gi3(0)
    gw(0)
    gp2(3)
    gw(1)
    gw(2)
    ca2(3)
    gi2(1)
    gi_b(3)
    gi_a(3)
    gi_c(3)
    gi3(1)
    gi2(2)
    gw(3)
    gw(4)
    gw(5)
    gi3(3)
    gi3(2)

    for store in stores + gw_stores[-2:]:
        store.wait()
    for copy in unsent.values():
        copy.wait_send()


def exchange(inputs, weight, cotangent):
    hbm = pl.BlockSpec(memory_space=pl.ANY)
    return pl.pallas_call(
        kernel,
        out_shape=(
            jax.ShapeDtypeStruct((CHUNKS, ROWS, COLS), BF16),
            jax.ShapeDtypeStruct((2, CHUNKS, ROWS, WIDTH), BF16),
            jax.ShapeDtypeStruct((COLS // GROUP, WIDTH, GROUP), BF16),
            jax.ShapeDtypeStruct((2, 8, ROWS, COLS), BF16),
            jax.ShapeDtypeStruct((WIDTH, 256), BF16),
        ),
        in_specs=[hbm] * 3,
        out_specs=(hbm,) * 5,
        scratch_shapes=[
            pltpu.VMEM((WIDTH, COLS), BF16),
            pltpu.VMEM((CHUNKS, 2, 8, ROWS, WIDTH), BF16),
            pltpu.VMEM((WIDTH, 256 * (CHUNKS - 1)), BF16),
            pltpu.VMEM((WIDTH, 256), BF16),
            pltpu.VMEM((2, 2, 8, ROWS, COLS), BF16),
            pltpu.VMEM((CHUNKS, 8, ROWS, COLS), BF16),
            pltpu.VMEM((CHUNKS, 2, 2, ROWS, A_WIDE), BF16),
            pltpu.VMEM((CHUNKS, 2, 2, ROWS, A_COLS), BF16),
            pltpu.VMEM((CHUNKS, 2, ROWS, A_COLS), BF16),
            pltpu.VMEM((CHUNKS, ROWS, A_COLS), BF16),
            pltpu.VMEM((CHUNKS, 4, ROWS, B_COLS), BF16),
            pltpu.VMEM((CHUNKS, 4, ROWS, B_COLS), BF16),
            pltpu.VMEM((CHUNKS, 2, ROWS, B_WIDE), BF16),
            pltpu.VMEM((CHUNKS, 2, ROWS, B_COLS), BF16),
            pltpu.VMEM((CHUNKS, 2, 8, ROWS, COLS), BF16),
            pltpu.VMEM((2, 256, WIDTH), F32),
            pltpu.VMEM((CHUNKS, 2, 2, 4, ROWS, WIDTH), BF16),
            pltpu.VMEM((CHUNKS - 1, 3, 2, 2, ROWS, WIDTH), BF16),
            pltpu.VMEM((7, 2, ROWS, WIDTH), BF16),
            pltpu.VMEM((CHUNKS - 1, 2, 2, ROWS, WIDTH), BF16),
            pltpu.VMEM((CHUNKS - 1, 2, ROWS, WIDTH), BF16),
            pltpu.VMEM((2, WIDTH, GROUP), BF16),
            pltpu.VMEM((CHUNKS, ROWS, COLS), BF16),
            pltpu.VMEM((CHUNKS, ROWS, COLS), BF16),
            pltpu.VMEM((2, CHUNKS, ROWS, WIDTH), BF16),
            pltpu.SemaphoreType.DMA((SLOTS,)),
            pltpu.SemaphoreType.DMA((SLOTS,)),
            pltpu.SemaphoreType.DMA((22,)),
        ],
        compiler_params=pltpu.CompilerParams(
            collective_id=0, has_side_effects=True, vmem_limit_bytes=61 * 2**20
        ),
        cost_estimate=pl.CostEstimate(flops=5 * 1024 * WIDTH * COLS, bytes_accessed=24 * 2**20, transcendentals=0),
        name="exchange",
    )(inputs.reshape(2, CHUNKS, ROWS, WIDTH), weight, cotangent.reshape(CHUNKS, ROWS, COLS))


def last_tokens(
    sum_hbm, x_hbm, g_hbm, act_hbm, gi_hbm, o_hbm, act_out, gi_out,
    total, x_t, grads, act, gi, sem, out_sem,
):
    groups = COLS // GROUP
    tokens = pltpu.make_async_copy(x_hbm, x_t, sem.at[0])
    tokens.start()
    loads = []
    for g in range(groups):
        cols = slice(g * GROUP, (g + 1) * GROUP)
        pair = (
            pltpu.make_async_copy(g_hbm.at[:, :, :, cols], grads.at[:, :, :, cols], sem.at[1 + g]),
            pltpu.make_async_copy(sum_hbm.at[g], total.at[g], sem.at[1 + groups + g]),
        )
        for load in pair:
            load.start()
        loads.append(pair)
    small = (
        (pltpu.make_async_copy(act_hbm, act, sem.at[1 + 2 * groups]), act, act_out),
        (pltpu.make_async_copy(gi_hbm, gi, sem.at[2 + 2 * groups]), gi, gi_out),
    )
    for load, _, _ in small:
        load.start()
    tokens.wait()
    stores = []
    for g in range(groups):
        for load in loads[g]:
            load.wait()

        @pl.loop(0, GROUP // TILE)
        def _(j):
            here = pl.ds(pl.multiple_of(j * TILE, TILE), TILE)
            cols = pl.ds(pl.multiple_of(g * GROUP + j * TILE, TILE), TILE)
            more = jnp.dot(
                x_t[...], grads[:, :, :, cols].reshape(256, TILE), preferred_element_type=F32
            )
            total[g, :, here] = (total[g, :, here].astype(F32) + more).astype(BF16)

        store = pltpu.make_async_copy(total.at[g], o_hbm.at[:, g * GROUP : (g + 1) * GROUP], out_sem.at[g])
        store.start()
        stores.append(store)
    for n, (load, held, out) in enumerate(small):
        load.wait()
        store = pltpu.make_async_copy(held, out, out_sem.at[groups + n])
        store.start()
        stores.append(store)
    for store in stores:
        store.wait()


def add_last(partial, tokens, grads, activated, grad_input):
    hbm = pl.BlockSpec(memory_space=pl.ANY)
    groups = COLS // GROUP
    return pl.pallas_call(
        last_tokens,
        out_shape=(
            jax.ShapeDtypeStruct((WIDTH, COLS), BF16),
            jax.ShapeDtypeStruct(activated.shape, BF16),
            jax.ShapeDtypeStruct(grad_input.shape, BF16),
        ),
        in_specs=[hbm] * 5,
        out_specs=(hbm, hbm, hbm),
        scratch_shapes=[
            pltpu.VMEM((groups, WIDTH, GROUP), BF16),
            pltpu.VMEM((WIDTH, 256), BF16),
            pltpu.VMEM((2, 8, ROWS, COLS), BF16),
            pltpu.VMEM(activated.shape, BF16),
            pltpu.VMEM(grad_input.shape, BF16),
            pltpu.SemaphoreType.DMA((3 + 2 * groups,)),
            pltpu.SemaphoreType.DMA((groups + 2,)),
        ],
        compiler_params=pltpu.CompilerParams(vmem_limit_bytes=60 * 2**20),
        cost_estimate=pl.CostEstimate(flops=2 * 256 * WIDTH * COLS, bytes_accessed=24 * 2**20, transcendentals=0),
        name="add_last",
    )(partial, tokens, grads, activated, grad_input)


def shards(inputs, weight, cotangent):
    activated, grad_input, partial, grads, tokens = exchange(inputs, weight, cotangent)
    grad_weight, activated, grad_input = add_last(partial, tokens, grads, activated, grad_input)
    return activated.reshape(64, COLS), grad_input.reshape(128, WIDTH), grad_weight


def solution(mesh):
    return jax.shard_map(
        shards,
        mesh=mesh,
        in_specs=(P("col", "row"), P("row", "col"), P("row", "col")),
        out_specs=(P("row", "col"), P("col", "row"), P("row", "col")),
        check_vma=False,
    )
```

```python
import jax
import jax.numpy as jnp
from jax import lax
from jax.experimental import pallas as pl
from jax.experimental.pallas import tpu as pltpu
from jax.sharding import PartitionSpec as P

MESH = pl.DeviceIdType.MESH
F32 = jnp.float32
BF16 = jnp.bfloat16

root_coef = 0.7978845608
cube_coef = 0.044715

CHUNKS = 4
LAST = CHUNKS - 1
ROWS = 16
WIDTH = 768
COLS = 6144
TILE = 512
A_COLS = 3584
B_COLS = COLS - A_COLS
A = slice(0, A_COLS)
B = slice(A_COLS, COLS)
A_HALF = (slice(0, 1536), slice(1536, A_COLS))
B_HALF = (slice(0, 1536), slice(1536, B_COLS))
A_WIDE = 2048
B_WIDE = 1536
GROUP = 1024
WAYS = (0, 1)
HOPS = (1, 2, 3)
SLOTS = 224


def width(cols):
    return cols.stop - cols.start


def in_b(cols):
    return slice(A_COLS + cols.start, A_COLS + cols.stop)


def kernel(
    x_hbm, w_hbm, cot_hbm,
    act_out, gi_out, gw_hbm, g_out, x_out,
    w, xs, xt, xt_last, part, share, ah, ra, ta, ay, rb, tb, bh, rbx, grad, acc, gi, rz, rd, ti, ry, stage, cot_ref, act_ref, gi_ref,
    send_sem, recv_sem, local_sem,
):
    row, col = lax.axis_index("row"), lax.axis_index("col")
    yhi, x, core = row // 8, (row // 2) % 4, row % 2
    ylo, z = col // 4, col % 4
    me = row // 2

    def device(yhi=yhi, x=x, core=core, ylo=ylo, z=z):
        return (yhi * 8 + x * 2 + core, ylo * 4 + z)

    y_peer = device(yhi=1 - yhi)
    core_peer = device(core=1 - core)
    ylo_peer = device(ylo=1 - ylo)
    near = (lax.rem(x + 1, 4), lax.rem(x + 3, 4))
    far = lax.rem(x + 2, 4)
    x_peer = tuple(device(x=at) for at in near)
    z_at = {d: lax.rem(z + d, 4) for d in HOPS}
    z_peer = {d: device(z=z_at[d]) for d in HOPS}
    both_peer = {d: device(ylo=1 - ylo, z=z_at[d]) for d in HOPS}
    peers = [y_peer, core_peer, ylo_peer, *x_peer, *z_peer.values(), *both_peer.values()]

    load_x = [
        pltpu.make_async_copy(x_hbm.at[:, k], xs.at[k, :, col], local_sem.at[9 + k]) for k in range(CHUNKS)
    ]
    load_w = pltpu.make_async_copy(w_hbm, w, local_sem.at[0])
    load_cot = pltpu.make_async_copy(cot_hbm, cot_ref, local_sem.at[13])
    for load in (*load_x, load_w, load_cot):
        load.start()

    barrier = pltpu.get_barrier_semaphore()
    for peer in peers:
        pl.semaphore_signal(barrier, inc=1, device_id=peer, device_id_type=MESH)
    pl.semaphore_wait(barrier, len(peers))

    copies = {}
    unsent = {}
    stores = []
    gw_stores = []

    def send(k, name, src, dst, peer):
        slot = len(copies)
        copy = pltpu.make_async_remote_copy(
            src_ref=src, dst_ref=dst, send_sem=send_sem.at[slot], recv_sem=recv_sem.at[slot],
            device_id=peer, device_id_type=MESH,
        )
        copy.start()
        copies[k, name] = unsent[k, name] = copy

    def sent(k, *names):
        for name in names:
            unsent.pop((k, name)).wait_send()

    def arrived(k, *names):
        for name in names:
            copies[k, name].wait_recv()

    def each(name, of):
        return [(name, d) for d in of]

    def tiles(first, last, body):
        @pl.loop(first // TILE, last // TILE)
        def _(j):
            body(pl.ds(pl.multiple_of(j * TILE, TILE), TILE))

    def rows4(k):
        return share.at[k].reshape(2, 4, ROWS, COLS)

    def x_start(k):
        send(k, "xy", x_hbm.at[:, k], xs.at[k, :, col], ylo_peer)
        for d in (1, 3, 2):
            send(k, ("xz", d), x_hbm.at[:, k], xs.at[k, :, col], z_peer[d])
        if k == 0:
            for d in (1, 3, 2):
                send(k, ("xf", d), x_hbm.at[:, k], xs.at[k, :, col], both_peer[d])

    def x_forward(k):
        arrived(k, "xy")
        block = xs.at[k, :, (1 - ylo) * 4 + z]
        for d in (1, 3, 2):
            send(k, ("xf", d), block, block, z_peer[d])

    waited = set()

    def prod_a(k, h):
        product(k, ("cA", h), A_HALF[h])

    def prod_b(k, h):
        product(k, ("cB", h), in_b(B_HALF[h]))

    def product(k, name, cols):
        if not waited:
            load_w.wait()
        if k not in waited:
            waited.add(k)
            load_x[k].wait()
            arrived(k, *(["xy"] if k == 0 else []), *each("xz", HOPS), *each("xf", HOPS))
        if k >= 2:
            sent(k - 2, name)

        def body(tile):
            out = jnp.dot(xs[k].reshape(256, WIDTH), w[:, tile], preferred_element_type=F32)
            part[k % 2, :, :, :, tile] = out.astype(BF16).reshape(2, 8, ROWS, TILE)

        tiles(cols.start, cols.stop, body)
        send(k, name, part.at[k % 2, 1 - core, :, :, cols], share.at[k, :, :, cols], core_peer)

    def add_cores(k, name, cols):
        arrived(k, name)

        def body(tile):
            mine = part[k % 2, core, :, :, tile].astype(F32)
            share[k, :, :, tile] = (mine + share[k, :, :, tile].astype(F32)).astype(BF16)

        tiles(cols.start, cols.stop, body)

    def ra1(k, h):
        cols = A_HALF[h]
        add_cores(k, ("cA", h), cols)
        n = width(cols)
        send(k, ("ah", h), rows4(k).at[:, far, :, cols], ah.at[k, h, :, :, 0:n], x_peer[h])
        send(k, ("an", 1 - h), rows4(k).at[:, near[1 - h], :, cols], ra.at[k, 1 - h, :, :, cols], x_peer[1 - h])

    def ra2(k, h):
        cols = A_HALF[h]
        arrived(k, ("ah", h))
        for y in (0, 1):
            at = y * 4 + near[h]
            total = share[k, at, :, cols].astype(F32) + ah[k, h, y, :, 0 : width(cols)].astype(F32)
            share[k, at, :, cols] = total.astype(BF16)
        send(k, ("am", h), rows4(k).at[:, near[h], :, cols], ra.at[k, h, :, :, cols], x_peer[h])

    def ra3(k):
        arrived(k, *each("an", WAYS), *each("am", WAYS))

        def body(tile):
            for y in (0, 1):
                total = share[k, y * 4 + x, :, tile].astype(F32)
                total += ra[k, 0, y, :, tile].astype(F32) + ra[k, 1, y, :, tile].astype(F32)
                ta[k, y, :, tile] = total.astype(BF16)

        tiles(0, A_COLS, body)
        send(k, "ay", ta.at[k, 1 - yhi], ay.at[k], y_peer)

    def rb1(k, h):
        cols = B_HALF[h]
        add_cores(k, ("cB", h), in_b(cols))
        send(k, ("by", h), share.at[k, pl.ds((1 - yhi) * 4, 4), :, in_b(cols)], rb.at[k, :, :, cols], y_peer)

    def rb2(k, h):
        cols = B_HALF[h]
        arrived(k, ("by", h))
        for at in range(4):
            total = share[k, yhi * 4 + at, :, in_b(cols)].astype(F32) + rb[k, at, :, cols].astype(F32)
            tb[k, at, :, cols] = total.astype(BF16)
        send(k, ("bh", h), tb.at[k, far, :, cols], bh.at[k, h, :, 0 : width(cols)], x_peer[h])
        send(k, ("bn", 1 - h), tb.at[k, near[1 - h], :, cols], rbx.at[k, 1 - h, :, cols], x_peer[1 - h])

    def rb3(k, h):
        cols = B_HALF[h]
        arrived(k, ("bh", h))
        total = tb[k, near[h], :, cols].astype(F32) + bh[k, h, :, 0 : width(cols)].astype(F32)
        tb[k, near[h], :, cols] = total.astype(BF16)
        send(k, ("bm", h), tb.at[k, near[h], :, cols], rbx.at[k, h, :, cols], x_peer[h])

    def activate(k, pre, cols):
        tangent = jnp.tanh(root_coef * (pre + cube_coef * pre * pre * pre))
        act_ref[k, :, cols] = (0.5 * pre * (1.0 + tangent)).astype(BF16)
        slope = 0.5 * (1.0 + tangent) + 0.5 * pre * (1.0 - tangent * tangent) * root_coef * (
            1.0 + 3.0 * cube_coef * pre * pre
        )
        grad[k, core, me, :, cols] = (cot_ref[k, :, cols].astype(F32) * slope).astype(BF16)

    def block(k, y, at, cols):
        return grad.at[k, core, y * 4 + at, :, cols]

    def pass_on(k, name, ref, peer):
        send(k, name, ref, ref, peer)

    activated = []

    def before_activate():
        if not activated:
            load_cot.wait()

    def after_activate(k):
        activated.append(k)
        if activated.count(k) == 2:
            store = pltpu.make_async_copy(act_ref.at[k], act_out.at[k], local_sem.at[14 + k])
            store.start()
            stores.append(store)

    def fin_a(k):
        arrived(k, "ay")
        before_activate()

        def body(tile):
            activate(k, ta[k, yhi, :, tile].astype(F32) + ay[k, :, tile].astype(F32), tile)

        tiles(0, A_COLS, body)
        after_activate(k)
        mine = block(k, yhi, x, A)
        pass_on(k, "gAy", mine, y_peer)
        for h in WAYS:
            pass_on(k, ("gA", h), mine, x_peer[h])

    def fin_b(k):
        arrived(k, *each("bn", WAYS), *each("bm", WAYS))
        before_activate()

        @pl.loop(0, B_COLS // TILE)
        def _(j):
            here = pl.ds(pl.multiple_of(j * TILE, TILE), TILE)
            pre = tb[k, x, :, here].astype(F32) + rbx[k, 0, :, here].astype(F32) + rbx[k, 1, :, here].astype(F32)
            activate(k, pre, pl.ds(pl.multiple_of(A_COLS + j * TILE, TILE), TILE))

        after_activate(k)
        mine = block(k, yhi, x, B)
        for h in WAYS:
            pass_on(k, ("gB", h), mine, x_peer[h])
        pass_on(k, "gBy", mine, y_peer)

    def relay(k, name, y, halves):
        for h in WAYS:
            pass_on(k, (name, h), block(k, y, near[1 - h], halves[h]), x_peer[h])

    def ga1(k):
        arrived(k, *each("gA", WAYS))
        relay(k, "gAr", yhi, A_HALF)

    def gp1(k):
        arrived(k, "gAy")
        for h in WAYS:
            pass_on(k, ("gP", h), block(k, 1 - yhi, x, A), x_peer[h])
        if k == LAST:
            pass_on(k, ("oA", 1), block(k, 1 - yhi, x, A), core_peer)

    def gp2(k):
        arrived(k, *each("gP", WAYS))
        relay(k, "gPr", 1 - yhi, A_HALF)
        if k == LAST:
            for h in WAYS:
                pass_on(k, ("oA", 2 + h), block(k, 1 - yhi, near[h], A), core_peer)

    def gb1(k):
        arrived(k, *each("gB", WAYS))
        relay(k, "gBr", yhi, [in_b(cols) for cols in B_HALF])
        for h in WAYS:
            pass_on(k, ("gBz", h), block(k, yhi, near[h], B), y_peer)

    def to_core(k, name, y, cols):
        pass_on(k, name, grad.at[k, core, pl.ds(y * 4, 4), :, cols], core_peer)

    def gb2(k):
        arrived(k, *each("gBr", WAYS))
        pass_on(k, "gBy2", block(k, yhi, far, B), y_peer)
        to_core(k, ("oB", 0), yhi, B)

    def ca1(k):
        arrived(k, *each("gAr", WAYS))
        to_core(k, ("oA", 0), yhi, A)

    def ca2(k):
        arrived(k, *each("gPr", WAYS))
        if k == LAST:
            pass_on(k, ("oA", 4), block(k, 1 - yhi, far, A), core_peer)
        else:
            to_core(k, ("oA", 1), 1 - yhi, A)

    def cb2(k):
        arrived(k, "gBy", *each("gBz", WAYS), "gBy2")
        to_core(k, ("oB", 1), 1 - yhi, B)

    def multiply_back(k, first, last, cols):
        def body(n):
            at = pl.ds(pl.multiple_of(n * 256, 256), 256)
            out = lax.dot_general(
                grad[k, :, :, :, cols].reshape(256, width(cols)), w[at, cols],
                (((1,), (1,)), ((), ())), preferred_element_type=F32,
            )
            if cols == B:
                acc[k % 2, :, at] = out
            else:
                out += acc[k % 2, :, at]
                gi[k, :, :, :, :, at] = out.astype(BF16).reshape(2, 2, 4, ROWS, 256)

        pl.loop(first, last)(body)

    def gi_b(k):
        arrived(k, *each("oB", WAYS))
        multiply_back(k, 0, WIDTH // 256, B)

    def gi_a(k):
        arrived(k, *each("oA", WAYS if k < LAST else range(5)))
        if k < LAST:
            multiply_back(k, 0, WIDTH // 256, A)
            for d in (1, 3, 2):
                send(k, ("iz", d), gi.at[k, :, :, z_at[d]], rz.at[k, d - 1], z_peer[d])
        else:
            store = pltpu.make_async_copy(grad.at[k], g_out, local_sem.at[1])
            store.start()
            stores.append(store)
            multiply_back(k, 0, 1, A)
            last_out(0, slice(0, 256))

    def gi_c(k):
        multiply_back(k, 1, WIDTH // 256, A)
        last_out(1, slice(256, WIDTH))
        xt_last[...] = xs[k].reshape(256, WIDTH).T
        store = pltpu.make_async_copy(xt_last, x_out, local_sem.at[8])
        store.start()
        stores.append(store)

    def last_out(s, cols):
        k = LAST
        for d in (2, 1, 3):
            send(k, ("iz", d, s), gi.at[k, :, ylo, z_at[d], :, cols], rd.at[d - 1, :, :, cols], z_peer[d])
            send(k, ("id", d, s), gi.at[k, :, 1 - ylo, z_at[d], :, cols], rd.at[2 + d, :, :, cols], both_peer[d])
        send(k, ("iy", s), gi.at[k, :, 1 - ylo, z, :, cols], rd.at[6, :, :, cols], ylo_peer)

    def gi2(k):
        arrived(k, *each("iz", HOPS))
        total = gi[k, :, :, z].astype(F32)
        for d in range(3):
            total += rz[k, d].astype(F32)
        ti[k] = total.astype(BF16)
        send(k, "iy", ti.at[k, :, 1 - ylo], ry.at[k], ylo_peer)

    def gi3(k):
        if k < LAST:
            arrived(k, "iy")
            total = ti[k, :, ylo].astype(F32) + ry[k].astype(F32)
        else:
            for s in WAYS:
                arrived(k, ("iy", s), *[(n, d, s) for n in ("iz", "id") for d in HOPS])
            total = gi[k, :, ylo, z].astype(F32)
            for d in range(7):
                total += rd[d].astype(F32)
        gi_ref[:, k] = total.astype(BF16)
        store = pltpu.make_async_copy(gi_ref.at[:, k], gi_out.at[:, k], local_sem.at[18 + k])
        store.start()
        stores.append(store)

    def gw(g):
        slot = g % 2
        if g == 0:
            xt[...] = xs[0 : CHUNKS - 1].reshape(256 * (CHUNKS - 1), WIDTH).T
        if g >= 2:
            gw_stores[g - 2].wait()

        @pl.loop(0, GROUP // TILE)
        def _(j):
            cols = pl.ds(pl.multiple_of(g * GROUP + j * TILE, TILE), TILE)
            out = jnp.dot(
                xt[...], grad[0 : CHUNKS - 1, :, :, :, cols].reshape(256 * (CHUNKS - 1), TILE),
                preferred_element_type=F32,
            )
            stage[slot, :, pl.ds(pl.multiple_of(j * TILE, TILE), TILE)] = out.astype(BF16)

        store = pltpu.make_async_copy(
            stage.at[slot], gw_hbm.at[g], local_sem.at[2 + g]
        )
        store.start()
        gw_stores.append(store)

    def drain():
        for copy in unsent.values():
            copy.wait_send()

    x_start(0)
    x_start(1)
    prod_b(0, 1)
    prod_a(0, 0)
    prod_b(0, 0)
    x_forward(1)
    rb1(0, 1)
    prod_a(0, 1)
    ra1(0, 0)
    x_start(2)
    rb1(0, 0)
    prod_a(1, 0)
    ra1(0, 1)
    prod_b(1, 1)
    rb2(0, 1)
    ra2(0, 0)
    x_forward(2)
    prod_b(1, 0)
    ra1(1, 0)
    prod_a(1, 1)
    rb3(0, 1)
    rb2(0, 0)
    rb1(1, 1)
    x_start(3)
    rb1(1, 0)
    ra2(0, 1)
    prod_b(2, 1)
    prod_b(2, 0)
    prod_a(2, 0)
    rb1(2, 1)
    ra1(1, 1)
    prod_a(2, 1)
    rb1(2, 0)
    ra2(1, 0)
    x_forward(3)
    ra1(2, 0)
    ra3(0)
    rb3(0, 0)
    ra1(2, 1)
    rb2(1, 1)
    ra2(1, 1)
    prod_a(3, 0)
    prod_b(3, 1)
    prod_b(3, 0)
    rb3(1, 1)
    fin_b(0)
    prod_a(3, 1)
    rb1(3, 1)
    ra1(3, 0)
    rb1(3, 0)
    rb2(2, 1)
    rb2(1, 0)
    ra2(2, 0)
    fin_a(0)
    ra1(3, 1)
    ra2(2, 1)
    ra3(1)
    rb3(2, 1)
    gb1(0)
    rb3(1, 0)
    rb2(2, 0)
    ra2(3, 0)
    rb2(3, 1)
    gb2(0)
    fin_b(1)
    gp1(0)
    rb3(2, 0)
    ga1(0)
    ra2(3, 1)
    ra3(2)
    rb3(3, 1)
    fin_a(1)
    rb2(3, 0)
    cb2(0)
    fin_b(2)
    ca1(0)
    gb1(1)
    gi_b(0)
    gp1(1)
    fin_a(2)
    rb3(3, 0)
    gp2(0)
    gb2(1)
    ga1(1)
    ra3(3)
    gb1(2)
    gp1(2)
    fin_b(3)
    cb2(1)
    ca2(0)
    gi_b(1)
    gb2(2)
    ga1(2)
    gp2(1)
    ca1(1)
    gi_a(0)
    gb1(3)
    gp2(2)
    fin_a(3)
    cb2(2)
    ca1(2)
    ca2(1)
    gi_b(2)
    gb2(3)
    ca2(2)
    gi2(0)
    ga1(3)
    gi_a(1)
    gp1(3)
    gi_a(2)
    cb2(3)
    ca1(3)
    gi3(0)
    gw(0)
    gp2(3)
    gw(1)
    ca2(3)
    gi2(1)
    gi_b(3)
    gi_a(3)
    gi_c(3)
    gw(2)
    gi3(1)
    gi2(2)
    gw(3)
    gw(4)
    gw(5)
    gi3(2)
    drain()
    gi3(3)

    for store in stores + gw_stores[-2:]:
        store.wait()


def exchange(inputs, weight, cotangent):
    hbm = pl.BlockSpec(memory_space=pl.ANY)
    return pl.pallas_call(
        kernel,
        out_shape=(
            jax.ShapeDtypeStruct((CHUNKS, ROWS, COLS), BF16),
            jax.ShapeDtypeStruct((2, CHUNKS, ROWS, WIDTH), BF16),
            jax.ShapeDtypeStruct((COLS // GROUP, WIDTH, GROUP), BF16),
            jax.ShapeDtypeStruct((2, 8, ROWS, COLS), BF16),
            jax.ShapeDtypeStruct((WIDTH, 256), BF16),
        ),
        in_specs=[hbm] * 3,
        out_specs=(hbm,) * 5,
        scratch_shapes=[
            pltpu.VMEM((WIDTH, COLS), BF16),
            pltpu.VMEM((CHUNKS, 2, 8, ROWS, WIDTH), BF16),
            pltpu.VMEM((WIDTH, 256 * (CHUNKS - 1)), BF16),
            pltpu.VMEM((WIDTH, 256), BF16),
            pltpu.VMEM((2, 2, 8, ROWS, COLS), BF16),
            pltpu.VMEM((CHUNKS, 8, ROWS, COLS), BF16),
            pltpu.VMEM((CHUNKS, 2, 2, ROWS, A_WIDE), BF16),
            pltpu.VMEM((CHUNKS, 2, 2, ROWS, A_COLS), BF16),
            pltpu.VMEM((CHUNKS, 2, ROWS, A_COLS), BF16),
            pltpu.VMEM((CHUNKS, ROWS, A_COLS), BF16),
            pltpu.VMEM((CHUNKS, 4, ROWS, B_COLS), BF16),
            pltpu.VMEM((CHUNKS, 4, ROWS, B_COLS), BF16),
            pltpu.VMEM((CHUNKS, 2, ROWS, B_WIDE), BF16),
            pltpu.VMEM((CHUNKS, 2, ROWS, B_COLS), BF16),
            pltpu.VMEM((CHUNKS, 2, 8, ROWS, COLS), BF16),
            pltpu.VMEM((2, 256, WIDTH), F32),
            pltpu.VMEM((CHUNKS, 2, 2, 4, ROWS, WIDTH), BF16),
            pltpu.VMEM((CHUNKS - 1, 3, 2, 2, ROWS, WIDTH), BF16),
            pltpu.VMEM((7, 2, ROWS, WIDTH), BF16),
            pltpu.VMEM((CHUNKS - 1, 2, 2, ROWS, WIDTH), BF16),
            pltpu.VMEM((CHUNKS - 1, 2, ROWS, WIDTH), BF16),
            pltpu.VMEM((2, WIDTH, GROUP), BF16),
            pltpu.VMEM((CHUNKS, ROWS, COLS), BF16),
            pltpu.VMEM((CHUNKS, ROWS, COLS), BF16),
            pltpu.VMEM((2, CHUNKS, ROWS, WIDTH), BF16),
            pltpu.SemaphoreType.DMA((SLOTS,)),
            pltpu.SemaphoreType.DMA((SLOTS,)),
            pltpu.SemaphoreType.DMA((22,)),
        ],
        compiler_params=pltpu.CompilerParams(
            collective_id=0, has_side_effects=True, vmem_limit_bytes=61 * 2**20
        ),
        cost_estimate=pl.CostEstimate(flops=5 * 1024 * WIDTH * COLS, bytes_accessed=24 * 2**20, transcendentals=0),
        name="exchange",
    )(inputs.reshape(2, CHUNKS, ROWS, WIDTH), weight, cotangent.reshape(CHUNKS, ROWS, COLS))


def last_tokens(
    sum_hbm, x_hbm, g_hbm, act_hbm, gi_hbm, o_hbm, act_out, gi_out,
    total, x_t, grads, act, gi, sem, out_sem,
):
    groups = COLS // GROUP
    tokens = pltpu.make_async_copy(x_hbm, x_t, sem.at[0])
    tokens.start()
    loads = []
    for g in range(groups):
        cols = slice(g * GROUP, (g + 1) * GROUP)
        pair = (
            pltpu.make_async_copy(g_hbm.at[:, :, :, cols], grads.at[:, :, :, cols], sem.at[1 + g]),
            pltpu.make_async_copy(sum_hbm.at[g], total.at[g], sem.at[1 + groups + g]),
        )
        for load in pair:
            load.start()
        loads.append(pair)
    small = (
        (pltpu.make_async_copy(act_hbm, act, sem.at[1 + 2 * groups]), act, act_out),
        (pltpu.make_async_copy(gi_hbm, gi, sem.at[2 + 2 * groups]), gi, gi_out),
    )
    for load, _, _ in small:
        load.start()
    tokens.wait()
    stores = []
    for g in range(groups):
        for load in loads[g]:
            load.wait()

        @pl.loop(0, GROUP // TILE)
        def _(j):
            here = pl.ds(pl.multiple_of(j * TILE, TILE), TILE)
            cols = pl.ds(pl.multiple_of(g * GROUP + j * TILE, TILE), TILE)
            more = jnp.dot(
                x_t[...], grads[:, :, :, cols].reshape(256, TILE), preferred_element_type=F32
            )
            total[g, :, here] = (total[g, :, here].astype(F32) + more).astype(BF16)

        store = pltpu.make_async_copy(total.at[g], o_hbm.at[:, g * GROUP : (g + 1) * GROUP], out_sem.at[g])
        store.start()
        stores.append(store)
    for n, (load, held, out) in enumerate(small):
        load.wait()
        store = pltpu.make_async_copy(held, out, out_sem.at[groups + n])
        store.start()
        stores.append(store)
    for store in stores:
        store.wait()


def add_last(partial, tokens, grads, activated, grad_input):
    hbm = pl.BlockSpec(memory_space=pl.ANY)
    groups = COLS // GROUP
    return pl.pallas_call(
        last_tokens,
        out_shape=(
            jax.ShapeDtypeStruct((WIDTH, COLS), BF16),
            jax.ShapeDtypeStruct(activated.shape, BF16),
            jax.ShapeDtypeStruct(grad_input.shape, BF16),
        ),
        in_specs=[hbm] * 5,
        out_specs=(hbm, hbm, hbm),
        scratch_shapes=[
            pltpu.VMEM((groups, WIDTH, GROUP), BF16),
            pltpu.VMEM((WIDTH, 256), BF16),
            pltpu.VMEM((2, 8, ROWS, COLS), BF16),
            pltpu.VMEM(activated.shape, BF16),
            pltpu.VMEM(grad_input.shape, BF16),
            pltpu.SemaphoreType.DMA((3 + 2 * groups,)),
            pltpu.SemaphoreType.DMA((groups + 2,)),
        ],
        compiler_params=pltpu.CompilerParams(vmem_limit_bytes=60 * 2**20),
        cost_estimate=pl.CostEstimate(flops=2 * 256 * WIDTH * COLS, bytes_accessed=24 * 2**20, transcendentals=0),
        name="add_last",
    )(partial, tokens, grads, activated, grad_input)


def shards(inputs, weight, cotangent):
    activated, grad_input, partial, grads, tokens = exchange(inputs, weight, cotangent)
    grad_weight, activated, grad_input = add_last(partial, tokens, grads, activated, grad_input)
    return activated.reshape(64, COLS), grad_input.reshape(128, WIDTH), grad_weight


def solution(mesh):
    return jax.shard_map(
        shards,
        mesh=mesh,
        in_specs=(P("col", "row"), P("row", "col"), P("row", "col")),
        out_specs=(P("row", "col"), P("col", "row"), P("row", "col")),
        check_vma=False,
    )
```

```python
import jax
import jax.numpy as jnp
from jax import lax
from jax.experimental import pallas as pl
from jax.experimental.pallas import tpu as pltpu
from jax.sharding import PartitionSpec as P

MESH = pl.DeviceIdType.MESH
F32 = jnp.float32
BF16 = jnp.bfloat16

root_coef = 0.7978845608
cube_coef = 0.044715

CHUNKS = 4
LAST = CHUNKS - 1
ROWS = 16
WIDTH = 768
COLS = 6144
TILE = 512
A_COLS = 3584
B_COLS = COLS - A_COLS
A = slice(0, A_COLS)
B = slice(A_COLS, COLS)
A_HALF = (slice(0, 1536), slice(1536, A_COLS))
B_HALF = (slice(0, 1536), slice(1536, B_COLS))
A_WIDE = 2048
B_WIDE = 1536
GROUP = 1024
WAYS = (0, 1)
HOPS = (1, 2, 3)
SLOTS = 224


def width(cols):
    return cols.stop - cols.start


def in_b(cols):
    return slice(A_COLS + cols.start, A_COLS + cols.stop)


def kernel(
    x_hbm, w_hbm, cot_hbm,
    act_out, gi_out, gw_hbm, g_out, x_out,
    w, xs, xt, xt_last, part, share, ah, ra, ta, ay, rb, tb, bh, rbx, grad, acc, gi, rz, rd, ti, ry, stage, cot_ref, act_ref, gi_ref,
    send_sem, recv_sem, local_sem,
):
    row, col = lax.axis_index("row"), lax.axis_index("col")
    yhi, x, core = row // 8, (row // 2) % 4, row % 2
    ylo, z = col // 4, col % 4
    me = row // 2

    def device(yhi=yhi, x=x, core=core, ylo=ylo, z=z):
        return (yhi * 8 + x * 2 + core, ylo * 4 + z)

    y_peer = device(yhi=1 - yhi)
    core_peer = device(core=1 - core)
    ylo_peer = device(ylo=1 - ylo)
    near = (lax.rem(x + 1, 4), lax.rem(x + 3, 4))
    far = lax.rem(x + 2, 4)
    x_peer = tuple(device(x=at) for at in near)
    z_at = {d: lax.rem(z + d, 4) for d in HOPS}
    z_peer = {d: device(z=z_at[d]) for d in HOPS}
    both_peer = {d: device(ylo=1 - ylo, z=z_at[d]) for d in HOPS}
    peers = [y_peer, core_peer, ylo_peer, *x_peer, *z_peer.values(), *both_peer.values()]

    load_x = [
        pltpu.make_async_copy(x_hbm.at[:, k], xs.at[k, :, col], local_sem.at[9 + k]) for k in range(CHUNKS)
    ]
    load_w = pltpu.make_async_copy(w_hbm, w, local_sem.at[0])
    load_cot = pltpu.make_async_copy(cot_hbm, cot_ref, local_sem.at[13])
    for load in (*load_x, load_w, load_cot):
        load.start()

    barrier = pltpu.get_barrier_semaphore()
    for peer in peers:
        pl.semaphore_signal(barrier, inc=1, device_id=peer, device_id_type=MESH)
    pl.semaphore_wait(barrier, len(peers))

    copies = {}
    unsent = {}
    stores = []
    gw_stores = []

    def send(k, name, src, dst, peer):
        slot = len(copies)
        copy = pltpu.make_async_remote_copy(
            src_ref=src, dst_ref=dst, send_sem=send_sem.at[slot], recv_sem=recv_sem.at[slot],
            device_id=peer, device_id_type=MESH,
        )
        copy.start()
        copies[k, name] = unsent[k, name] = copy

    def sent(k, *names):
        for name in names:
            unsent.pop((k, name)).wait_send()

    def arrived(k, *names):
        for name in names:
            copies[k, name].wait_recv()

    def each(name, of):
        return [(name, d) for d in of]

    def tiles(first, last, body):
        @pl.loop(first // TILE, last // TILE)
        def _(j):
            body(pl.ds(pl.multiple_of(j * TILE, TILE), TILE))

    def rows4(k):
        return share.at[k].reshape(2, 4, ROWS, COLS)

    def x_start(k):
        send(k, "xy", x_hbm.at[:, k], xs.at[k, :, col], ylo_peer)
        for d in (1, 3, 2):
            send(k, ("xz", d), x_hbm.at[:, k], xs.at[k, :, col], z_peer[d])
        if k == 0:
            for d in (1, 3, 2):
                send(k, ("xf", d), x_hbm.at[:, k], xs.at[k, :, col], both_peer[d])

    def x_forward(k):
        arrived(k, "xy")
        block = xs.at[k, :, (1 - ylo) * 4 + z]
        for d in (1, 3, 2):
            send(k, ("xf", d), block, block, z_peer[d])

    waited = set()

    def prod_a(k, h):
        product(k, ("cA", h), A_HALF[h])

    def prod_b(k, h):
        product(k, ("cB", h), in_b(B_HALF[h]))

    def product(k, name, cols):
        if not waited:
            load_w.wait()
        if k not in waited:
            waited.add(k)
            load_x[k].wait()
            arrived(k, *(["xy"] if k == 0 else []), *each("xz", HOPS), *each("xf", HOPS))
        if k >= 2:
            sent(k - 2, name)

        def body(tile):
            out = jnp.dot(xs[k].reshape(256, WIDTH), w[:, tile], preferred_element_type=F32)
            part[k % 2, :, :, :, tile] = out.astype(BF16).reshape(2, 8, ROWS, TILE)

        tiles(cols.start, cols.stop, body)
        send(k, name, part.at[k % 2, 1 - core, :, :, cols], share.at[k, :, :, cols], core_peer)

    def add_cores(k, name, cols):
        arrived(k, name)

        def body(tile):
            mine = part[k % 2, core, :, :, tile].astype(F32)
            share[k, :, :, tile] = (mine + share[k, :, :, tile].astype(F32)).astype(BF16)

        tiles(cols.start, cols.stop, body)

    def ra1(k, h):
        cols = A_HALF[h]
        add_cores(k, ("cA", h), cols)
        n = width(cols)
        send(k, ("ah", h), rows4(k).at[:, far, :, cols], ah.at[k, h, :, :, 0:n], x_peer[h])
        send(k, ("an", 1 - h), rows4(k).at[:, near[1 - h], :, cols], ra.at[k, 1 - h, :, :, cols], x_peer[1 - h])

    def ra2(k, h):
        cols = A_HALF[h]
        arrived(k, ("ah", h))
        for y in (0, 1):
            at = y * 4 + near[h]
            total = share[k, at, :, cols].astype(F32) + ah[k, h, y, :, 0 : width(cols)].astype(F32)
            share[k, at, :, cols] = total.astype(BF16)
        send(k, ("am", h), rows4(k).at[:, near[h], :, cols], ra.at[k, h, :, :, cols], x_peer[h])

    def ra3(k):
        arrived(k, *each("an", WAYS), *each("am", WAYS))

        def body(tile):
            for y in (0, 1):
                total = share[k, y * 4 + x, :, tile].astype(F32)
                total += ra[k, 0, y, :, tile].astype(F32) + ra[k, 1, y, :, tile].astype(F32)
                ta[k, y, :, tile] = total.astype(BF16)

        tiles(0, A_COLS, body)
        send(k, "ay", ta.at[k, 1 - yhi], ay.at[k], y_peer)

    def rb1(k, h):
        cols = B_HALF[h]
        add_cores(k, ("cB", h), in_b(cols))
        send(k, ("by", h), share.at[k, pl.ds((1 - yhi) * 4, 4), :, in_b(cols)], rb.at[k, :, :, cols], y_peer)

    def rb2(k, h):
        cols = B_HALF[h]
        arrived(k, ("by", h))
        for at in range(4):
            total = share[k, yhi * 4 + at, :, in_b(cols)].astype(F32) + rb[k, at, :, cols].astype(F32)
            tb[k, at, :, cols] = total.astype(BF16)
        send(k, ("bh", h), tb.at[k, far, :, cols], bh.at[k, h, :, 0 : width(cols)], x_peer[h])
        send(k, ("bn", 1 - h), tb.at[k, near[1 - h], :, cols], rbx.at[k, 1 - h, :, cols], x_peer[1 - h])

    def rb3(k, h):
        cols = B_HALF[h]
        arrived(k, ("bh", h))
        total = tb[k, near[h], :, cols].astype(F32) + bh[k, h, :, 0 : width(cols)].astype(F32)
        tb[k, near[h], :, cols] = total.astype(BF16)
        send(k, ("bm", h), tb.at[k, near[h], :, cols], rbx.at[k, h, :, cols], x_peer[h])

    def activate(k, pre, cols):
        tangent = jnp.tanh(root_coef * (pre + cube_coef * pre * pre * pre))
        act_ref[k, :, cols] = (0.5 * pre * (1.0 + tangent)).astype(BF16)
        slope = 0.5 * (1.0 + tangent) + 0.5 * pre * (1.0 - tangent * tangent) * root_coef * (
            1.0 + 3.0 * cube_coef * pre * pre
        )
        grad[k, core, me, :, cols] = (cot_ref[k, :, cols].astype(F32) * slope).astype(BF16)

    def block(k, y, at, cols):
        return grad.at[k, core, y * 4 + at, :, cols]

    def pass_on(k, name, ref, peer):
        send(k, name, ref, ref, peer)

    activated = []

    def before_activate():
        if not activated:
            load_cot.wait()

    def after_activate(k):
        activated.append(k)
        if activated.count(k) == 2:
            store = pltpu.make_async_copy(act_ref.at[k], act_out.at[k], local_sem.at[14 + k])
            store.start()
            stores.append(store)

    def fin_a(k):
        arrived(k, "ay")
        before_activate()

        def body(tile):
            activate(k, ta[k, yhi, :, tile].astype(F32) + ay[k, :, tile].astype(F32), tile)

        tiles(0, A_COLS, body)
        after_activate(k)
        mine = block(k, yhi, x, A)
        pass_on(k, "gAy", mine, y_peer)
        for h in WAYS:
            pass_on(k, ("gA", h), mine, x_peer[h])

    def fin_b(k):
        arrived(k, *each("bn", WAYS), *each("bm", WAYS))
        before_activate()

        @pl.loop(0, B_COLS // TILE)
        def _(j):
            here = pl.ds(pl.multiple_of(j * TILE, TILE), TILE)
            pre = tb[k, x, :, here].astype(F32) + rbx[k, 0, :, here].astype(F32) + rbx[k, 1, :, here].astype(F32)
            activate(k, pre, pl.ds(pl.multiple_of(A_COLS + j * TILE, TILE), TILE))

        after_activate(k)
        mine = block(k, yhi, x, B)
        for h in WAYS:
            pass_on(k, ("gB", h), mine, x_peer[h])
        pass_on(k, "gBy", mine, y_peer)

    def relay(k, name, y, halves):
        for h in WAYS:
            pass_on(k, (name, h), block(k, y, near[1 - h], halves[h]), x_peer[h])

    def ga1(k):
        arrived(k, *each("gA", WAYS))
        relay(k, "gAr", yhi, A_HALF)

    def gp1(k):
        arrived(k, "gAy")
        for h in WAYS:
            pass_on(k, ("gP", h), block(k, 1 - yhi, x, A), x_peer[h])
        if k == LAST:
            pass_on(k, ("oA", 1), block(k, 1 - yhi, x, A), core_peer)

    def gp2(k):
        arrived(k, *each("gP", WAYS))
        relay(k, "gPr", 1 - yhi, A_HALF)
        if k == LAST:
            for h in WAYS:
                pass_on(k, ("oA", 2 + h), block(k, 1 - yhi, near[h], A), core_peer)

    def gb1(k):
        arrived(k, *each("gB", WAYS))
        relay(k, "gBr", yhi, [in_b(cols) for cols in B_HALF])
        for h in WAYS:
            pass_on(k, ("gBz", h), block(k, yhi, near[h], B), y_peer)

    def to_core(k, name, y, cols):
        pass_on(k, name, grad.at[k, core, pl.ds(y * 4, 4), :, cols], core_peer)

    def gb2(k):
        arrived(k, *each("gBr", WAYS))
        pass_on(k, "gBy2", block(k, yhi, far, B), y_peer)
        to_core(k, ("oB", 0), yhi, B)

    def ca1(k):
        arrived(k, *each("gAr", WAYS))
        to_core(k, ("oA", 0), yhi, A)

    def ca2(k):
        arrived(k, *each("gPr", WAYS))
        if k == LAST:
            pass_on(k, ("oA", 4), block(k, 1 - yhi, far, A), core_peer)
        else:
            to_core(k, ("oA", 1), 1 - yhi, A)

    def cb2(k):
        arrived(k, "gBy", *each("gBz", WAYS), "gBy2")
        to_core(k, ("oB", 1), 1 - yhi, B)

    def multiply_back(k, first, last, cols):
        def body(n):
            at = pl.ds(pl.multiple_of(n * 256, 256), 256)
            out = lax.dot_general(
                grad[k, :, :, :, cols].reshape(256, width(cols)), w[at, cols],
                (((1,), (1,)), ((), ())), preferred_element_type=F32,
            )
            if cols == B:
                acc[k % 2, :, at] = out
            else:
                out += acc[k % 2, :, at]
                gi[k, :, :, :, :, at] = out.astype(BF16).reshape(2, 2, 4, ROWS, 256)

        pl.loop(first, last)(body)

    def gi_b(k):
        arrived(k, *each("oB", WAYS))
        multiply_back(k, 0, WIDTH // 256, B)

    def gi_a(k):
        arrived(k, *each("oA", WAYS if k < LAST else range(5)))
        if k < LAST:
            multiply_back(k, 0, WIDTH // 256, A)
            for d in (1, 3, 2):
                send(k, ("iz", d), gi.at[k, :, :, z_at[d]], rz.at[k, d - 1], z_peer[d])
        else:
            store = pltpu.make_async_copy(grad.at[k], g_out, local_sem.at[1])
            store.start()
            stores.append(store)
            multiply_back(k, 0, 1, A)
            last_out(0, slice(0, 256))

    def gi_c(k):
        multiply_back(k, 1, WIDTH // 256, A)
        last_out(1, slice(256, WIDTH))
        xt_last[...] = xs[k].reshape(256, WIDTH).T
        store = pltpu.make_async_copy(xt_last, x_out, local_sem.at[8])
        store.start()
        stores.append(store)

    def last_out(s, cols):
        k = LAST
        for d in (2, 1, 3):
            send(k, ("iz", d, s), gi.at[k, :, ylo, z_at[d], :, cols], rd.at[d - 1, :, :, cols], z_peer[d])
            send(k, ("id", d, s), gi.at[k, :, 1 - ylo, z_at[d], :, cols], rd.at[2 + d, :, :, cols], both_peer[d])
        send(k, ("iy", s), gi.at[k, :, 1 - ylo, z, :, cols], rd.at[6, :, :, cols], ylo_peer)

    def gi2(k):
        arrived(k, *each("iz", HOPS))
        total = gi[k, :, :, z].astype(F32)
        for d in range(3):
            total += rz[k, d].astype(F32)
        ti[k] = total.astype(BF16)
        send(k, "iy", ti.at[k, :, 1 - ylo], ry.at[k], ylo_peer)

    def gi3(k):
        if k < LAST:
            arrived(k, "iy")
            total = ti[k, :, ylo].astype(F32) + ry[k].astype(F32)
        else:
            for s in WAYS:
                arrived(k, ("iy", s), *[(n, d, s) for n in ("iz", "id") for d in HOPS])
            total = gi[k, :, ylo, z].astype(F32)
            for d in range(7):
                total += rd[d].astype(F32)
        gi_ref[:, k] = total.astype(BF16)
        store = pltpu.make_async_copy(gi_ref.at[:, k], gi_out.at[:, k], local_sem.at[18 + k])
        store.start()
        stores.append(store)

    def gw(g):
        slot = g % 2
        if g == 0:
            xt[...] = xs[0 : CHUNKS - 1].reshape(256 * (CHUNKS - 1), WIDTH).T
        if g >= 2:
            gw_stores[g - 2].wait()

        @pl.loop(0, GROUP // TILE)
        def _(j):
            cols = pl.ds(pl.multiple_of(g * GROUP + j * TILE, TILE), TILE)
            out = jnp.dot(
                xt[...], grad[0 : CHUNKS - 1, :, :, :, cols].reshape(256 * (CHUNKS - 1), TILE),
                preferred_element_type=F32,
            )
            stage[slot, :, pl.ds(pl.multiple_of(j * TILE, TILE), TILE)] = out.astype(BF16)

        store = pltpu.make_async_copy(
            stage.at[slot], gw_hbm.at[g], local_sem.at[2 + g]
        )
        store.start()
        gw_stores.append(store)

    def drain():
        for copy in unsent.values():
            copy.wait_send()

    x_start(0)
    x_start(1)
    prod_b(0, 1)
    prod_a(0, 0)
    prod_b(0, 0)
    x_forward(1)
    rb1(0, 1)
    prod_a(0, 1)
    ra1(0, 0)
    x_start(2)
    rb1(0, 0)
    prod_a(1, 0)
    ra1(0, 1)
    prod_b(1, 1)
    rb2(0, 1)
    ra2(0, 0)
    x_forward(2)
    prod_b(1, 0)
    ra1(1, 0)
    prod_a(1, 1)
    rb3(0, 1)
    rb2(0, 0)
    rb1(1, 1)
    x_start(3)
    rb1(1, 0)
    ra2(0, 1)
    prod_b(2, 1)
    prod_b(2, 0)
    prod_a(2, 0)
    rb1(2, 1)
    ra1(1, 1)
    prod_a(2, 1)
    rb1(2, 0)
    ra2(1, 0)
    x_forward(3)
    ra1(2, 0)
    ra3(0)
    rb3(0, 0)
    ra1(2, 1)
    rb2(1, 1)
    ra2(1, 1)
    prod_a(3, 0)
    prod_b(3, 1)
    prod_b(3, 0)
    rb3(1, 1)
    fin_b(0)
    prod_a(3, 1)
    rb1(3, 1)
    ra1(3, 0)
    rb1(3, 0)
    rb2(2, 1)
    rb2(1, 0)
    ra2(2, 0)
    fin_a(0)
    ra1(3, 1)
    ra2(2, 1)
    ra3(1)
    rb3(2, 1)
    gb1(0)
    rb3(1, 0)
    rb2(2, 0)
    ra2(3, 0)
    rb2(3, 1)
    gb2(0)
    fin_b(1)
    gp1(0)
    rb3(2, 0)
    ga1(0)
    ra2(3, 1)
    ra3(2)
    rb3(3, 1)
    fin_a(1)
    rb2(3, 0)
    cb2(0)
    fin_b(2)
    ca1(0)
    gb1(1)
    gi_b(0)
    gp1(1)
    fin_a(2)
    rb3(3, 0)
    gp2(0)
    gb2(1)
    ga1(1)
    ra3(3)
    gb1(2)
    gp1(2)
    fin_b(3)
    cb2(1)
    ca2(0)
    gi_b(1)
    gb2(2)
    ga1(2)
    gp2(1)
    ca1(1)
    gi_a(0)
    gb1(3)
    gp2(2)
    fin_a(3)
    cb2(2)
    ca1(2)
    ca2(1)
    gi_b(2)
    gb2(3)
    ca2(2)
    gi2(0)
    ga1(3)
    gi_a(1)
    gp1(3)
    gi_a(2)
    cb2(3)
    ca1(3)
    gi3(0)
    gw(0)
    gp2(3)
    gw(1)
    gw(2)
    ca2(3)
    gi2(1)
    gi_b(3)
    gi_a(3)
    gi_c(3)
    gi3(1)
    gi2(2)
    gw(3)
    gw(4)
    gw(5)
    gi3(2)
    drain()
    gi3(3)

    for store in stores + gw_stores[-2:]:
        store.wait()


def exchange(inputs, weight, cotangent):
    hbm = pl.BlockSpec(memory_space=pl.ANY)
    return pl.pallas_call(
        kernel,
        out_shape=(
            jax.ShapeDtypeStruct((CHUNKS, ROWS, COLS), BF16),
            jax.ShapeDtypeStruct((2, CHUNKS, ROWS, WIDTH), BF16),
            jax.ShapeDtypeStruct((COLS // GROUP, WIDTH, GROUP), BF16),
            jax.ShapeDtypeStruct((2, 8, ROWS, COLS), BF16),
            jax.ShapeDtypeStruct((WIDTH, 256), BF16),
        ),
        in_specs=[hbm] * 3,
        out_specs=(hbm,) * 5,
        scratch_shapes=[
            pltpu.VMEM((WIDTH, COLS), BF16),
            pltpu.VMEM((CHUNKS, 2, 8, ROWS, WIDTH), BF16),
            pltpu.VMEM((WIDTH, 256 * (CHUNKS - 1)), BF16),
            pltpu.VMEM((WIDTH, 256), BF16),
            pltpu.VMEM((2, 2, 8, ROWS, COLS), BF16),
            pltpu.VMEM((CHUNKS, 8, ROWS, COLS), BF16),
            pltpu.VMEM((CHUNKS, 2, 2, ROWS, A_WIDE), BF16),
            pltpu.VMEM((CHUNKS, 2, 2, ROWS, A_COLS), BF16),
            pltpu.VMEM((CHUNKS, 2, ROWS, A_COLS), BF16),
            pltpu.VMEM((CHUNKS, ROWS, A_COLS), BF16),
            pltpu.VMEM((CHUNKS, 4, ROWS, B_COLS), BF16),
            pltpu.VMEM((CHUNKS, 4, ROWS, B_COLS), BF16),
            pltpu.VMEM((CHUNKS, 2, ROWS, B_WIDE), BF16),
            pltpu.VMEM((CHUNKS, 2, ROWS, B_COLS), BF16),
            pltpu.VMEM((CHUNKS, 2, 8, ROWS, COLS), BF16),
            pltpu.VMEM((2, 256, WIDTH), F32),
            pltpu.VMEM((CHUNKS, 2, 2, 4, ROWS, WIDTH), BF16),
            pltpu.VMEM((CHUNKS - 1, 3, 2, 2, ROWS, WIDTH), BF16),
            pltpu.VMEM((7, 2, ROWS, WIDTH), BF16),
            pltpu.VMEM((CHUNKS - 1, 2, 2, ROWS, WIDTH), BF16),
            pltpu.VMEM((CHUNKS - 1, 2, ROWS, WIDTH), BF16),
            pltpu.VMEM((2, WIDTH, GROUP), BF16),
            pltpu.VMEM((CHUNKS, ROWS, COLS), BF16),
            pltpu.VMEM((CHUNKS, ROWS, COLS), BF16),
            pltpu.VMEM((2, CHUNKS, ROWS, WIDTH), BF16),
            pltpu.SemaphoreType.DMA((SLOTS,)),
            pltpu.SemaphoreType.DMA((SLOTS,)),
            pltpu.SemaphoreType.DMA((22,)),
        ],
        compiler_params=pltpu.CompilerParams(
            collective_id=0, has_side_effects=True, vmem_limit_bytes=61 * 2**20
        ),
        cost_estimate=pl.CostEstimate(flops=5 * 1024 * WIDTH * COLS, bytes_accessed=24 * 2**20, transcendentals=0),
        name="exchange",
    )(inputs.reshape(2, CHUNKS, ROWS, WIDTH), weight, cotangent.reshape(CHUNKS, ROWS, COLS))


def last_tokens(
    sum_hbm, x_hbm, g_hbm, act_hbm, gi_hbm, o_hbm, act_out, gi_out,
    total, x_t, grads, act, gi, sem, out_sem,
):
    groups = COLS // GROUP
    tokens = pltpu.make_async_copy(x_hbm, x_t, sem.at[0])
    tokens.start()
    loads = []
    for g in range(groups):
        cols = slice(g * GROUP, (g + 1) * GROUP)
        pair = (
            pltpu.make_async_copy(g_hbm.at[:, :, :, cols], grads.at[:, :, :, cols], sem.at[1 + g]),
            pltpu.make_async_copy(sum_hbm.at[g], total.at[g], sem.at[1 + groups + g]),
        )
        for load in pair:
            load.start()
        loads.append(pair)
    small = (
        (pltpu.make_async_copy(act_hbm, act, sem.at[1 + 2 * groups]), act, act_out),
        (pltpu.make_async_copy(gi_hbm, gi, sem.at[2 + 2 * groups]), gi, gi_out),
    )
    for load, _, _ in small:
        load.start()
    tokens.wait()
    stores = []
    for g in range(groups):
        for load in loads[g]:
            load.wait()

        @pl.loop(0, GROUP // TILE)
        def _(j):
            here = pl.ds(pl.multiple_of(j * TILE, TILE), TILE)
            cols = pl.ds(pl.multiple_of(g * GROUP + j * TILE, TILE), TILE)
            more = jnp.dot(
                x_t[...], grads[:, :, :, cols].reshape(256, TILE), preferred_element_type=F32
            )
            total[g, :, here] = (total[g, :, here].astype(F32) + more).astype(BF16)

        store = pltpu.make_async_copy(total.at[g], o_hbm.at[:, g * GROUP : (g + 1) * GROUP], out_sem.at[g])
        store.start()
        stores.append(store)
    for n, (load, held, out) in enumerate(small):
        load.wait()
        store = pltpu.make_async_copy(held, out, out_sem.at[groups + n])
        store.start()
        stores.append(store)
    for store in stores:
        store.wait()


def add_last(partial, tokens, grads, activated, grad_input):
    hbm = pl.BlockSpec(memory_space=pl.ANY)
    groups = COLS // GROUP
    return pl.pallas_call(
        last_tokens,
        out_shape=(
            jax.ShapeDtypeStruct((WIDTH, COLS), BF16),
            jax.ShapeDtypeStruct(activated.shape, BF16),
            jax.ShapeDtypeStruct(grad_input.shape, BF16),
        ),
        in_specs=[hbm] * 5,
        out_specs=(hbm, hbm, hbm),
        scratch_shapes=[
            pltpu.VMEM((groups, WIDTH, GROUP), BF16),
            pltpu.VMEM((WIDTH, 256), BF16),
            pltpu.VMEM((2, 8, ROWS, COLS), BF16),
            pltpu.VMEM(activated.shape, BF16),
            pltpu.VMEM(grad_input.shape, BF16),
            pltpu.SemaphoreType.DMA((3 + 2 * groups,)),
            pltpu.SemaphoreType.DMA((groups + 2,)),
        ],
        compiler_params=pltpu.CompilerParams(vmem_limit_bytes=60 * 2**20),
        cost_estimate=pl.CostEstimate(flops=2 * 256 * WIDTH * COLS, bytes_accessed=24 * 2**20, transcendentals=0),
        name="add_last",
    )(partial, tokens, grads, activated, grad_input)


def shards(inputs, weight, cotangent):
    activated, grad_input, partial, grads, tokens = exchange(inputs, weight, cotangent)
    grad_weight, activated, grad_input = add_last(partial, tokens, grads, activated, grad_input)
    return activated.reshape(64, COLS), grad_input.reshape(128, WIDTH), grad_weight


def solution(mesh):
    return jax.shard_map(
        shards,
        mesh=mesh,
        in_specs=(P("col", "row"), P("row", "col"), P("row", "col")),
        out_specs=(P("row", "col"), P("col", "row"), P("row", "col")),
        check_vma=False,
    )
```
